32 devices in a mesh: cuts: 2 (over y), row: 16 (over z, x, core).
Axes of the slice: x: 2, y: 2, z: 4, core: 2. Of those that a mesh axis runs over, the one named last changes fastest.
Arguments:
- block_tiles: float32 [48, 24, 128, 128], P('row'), may hold values from -0.109375 to 0.109375
- tile_pattern: int32 [48, 24], P('row'), may hold values from 0 to 47, as said below
- start_vectors: float32 [2, 32, 6144], P('cuts', None, 'row'), may hold values from -8 to 8
- centers: float32 [2], P('cuts'), may hold values from -0.3 to 0.3
- halfwidths: float32 [2], P('cuts'), may hold values from 0.9 to 1.3
- dup_pairs: int32 [2, 8, 2], P('cuts'), may hold values from 0 to 31, as said below
Outputs:
- filtered_basis: float32 [2, 32, 6144], P('cuts', None, 'row')
- projected: float32 [2, 32, 32], P('cuts')
The draws below stay inside these ranges and needn't reach their ends.
Inputs may be any that keep to these rules, and one draw needn't show every extreme that they name: tile_pattern[r, 0] = r; the other entries of block row r are distinct block rows, each within 12 of r cyclically and different from r. `dup_pairs`: within one slice the first entries of the pairs are distinct, and so are the second entries; the pairs of slice 0 are not used.
All inputs are finite; a program needn't handle non-finite values.
Results may differ from the reference program's by a relative error of at most 0.00015.
Values sent between devices are 32-bit elements; how exact they have to be, the bound alone decides.
No kernel may reach another device: no remote copies, remote signals or barrier semaphores. Data moves between devices by JAX's collectives and lax.ppermute only.
A program may use at most 64 MiB of HBM per device.

```python
import math
import jax
import jax.numpy as jnp
from jax import lax

B = 128
K = 24
V = 32
DEG = 8
REACH = 12
PAIRS = 8
SLICES = 2
NB = 48
ORDER = 6144


def pair_table(key):

    def draw_slice(slice_key):
        own_index = jax.random.permutation(jax.random.fold_in(slice_key, 1), V)[:PAIRS]
        their_index = jax.random.permutation(jax.random.fold_in(slice_key, 2), V)[:PAIRS]
        return jnp.stack([own_index, their_index], axis=1)
    slice_keys = jax.random.split(jax.random.fold_in(key, 7), SLICES)
    return jax.vmap(draw_slice)(slice_keys).astype(jnp.int32)


def draw_dup_pairs(key, part):
    return pair_table(key)


def draw_tile_pattern(key, part):

    def draw_row(row_key, row_index):
        chosen = jax.random.permutation(row_key, 2 * REACH)[:K - 1].astype(jnp.int32)
        offsets = jnp.where(chosen < REACH, chosen - REACH, chosen - REACH + 1)
        return jnp.concatenate([row_index[None], (row_index + offsets) % NB])
    row_keys = jax.random.split(jax.random.fold_in(key, 3), NB)
    row_ids = jnp.arange(NB, dtype=jnp.int32)
    return jax.vmap(draw_row)(row_keys, row_ids).astype(jnp.int32)


def draw_start_vectors(key, part):
    full_shape = (SLICES, V, ORDER)
    base_draw = jnp.clip(jax.random.normal(jax.random.fold_in(key, 11), full_shape, jnp.float32), -6.0, 6.0)
    pairs = pair_table(key)
    own_index = pairs[:, :, 0]
    their_index = pairs[:, :, 1]
    previous = jnp.roll(base_draw, 1, axis=0)
    echoed = jnp.take_along_axis(previous, their_index[:, :, None], axis=1)
    own_rows = jnp.take_along_axis(base_draw, own_index[:, :, None], axis=1)
    blended = 0.8 * echoed + 0.6 * own_rows
    slice_ids = jnp.arange(SLICES, dtype=jnp.int32)[:, None]
    target = jnp.where(slice_ids[:, :, None] > 0, blended, own_rows)
    return base_draw.at[slice_ids, own_index].set(target)


def steps_of(own_key, dims, pieces, smallest, largest):
    def one(dim, parts):
        draws = jax.random.uniform(jax.random.fold_in(jax.random.fold_in(own_key, 6), dim), (parts,), jnp.float32, smallest / len(pieces), largest / len(pieces))
        return jnp.repeat(jnp.exp(draws), dims[dim] // parts).reshape((-1,) + (1,) * (len(dims) - dim - 1))

    level = one(*pieces[0])
    for cut in pieces[1:]:
        level = level * one(*cut)
    return level


def noise(rng, shape, deviation, most, pieces=(), kind=jnp.bfloat16):
    drawn = deviation * jax.random.normal(rng, shape, jnp.float32)
    if pieces:
        drawn = drawn * steps_of(rng, shape, pieces, -0.22, 0.18)
    return jnp.clip(drawn, -most, most).astype(kind)


def setup_inputs(seed: int = 0) -> dict:
    keys = jax.random.split(jax.random.key(seed), 7)
    block_tiles = noise(keys[0], (NB, K, B, B), (K * B) ** -0.5, 0.109375, ((0, 16),), jnp.float32)
    tile_pattern = draw_tile_pattern(jax.random.fold_in(keys[6], 71), 0)
    start_vectors = draw_start_vectors(jax.random.fold_in(keys[6], 71), 0)
    centers = jnp.clip(jax.random.uniform(keys[3], (SLICES,), jnp.float32, -0.3, 0.3) * steps_of(keys[3], (SLICES,), ((0, 2),), -0.4, 0.0), -0.3, 0.3)
    halfwidths = jnp.clip(0.9 + 0.39999998 * jax.random.uniform(keys[4], (SLICES,), jnp.float32) ** steps_of(keys[4], (SLICES,), ((0, 2),), -0.2, 0.2), 0.9, 1.3)
    dup_pairs = draw_dup_pairs(jax.random.fold_in(keys[6], 71), 0)
    return {"block_tiles": block_tiles, "tile_pattern": tile_pattern, "start_vectors": start_vectors, "centers": centers, "halfwidths": halfwidths, "dup_pairs": dup_pairs}


def apply_all(vectors, block_tiles, tile_pattern):
    vec_count = vectors.shape[0]
    blocks = vectors.reshape(vec_count, NB, B)
    picked = jnp.take(blocks, tile_pattern, axis=1)
    product = jnp.einsum('vrkc,rkdc->vrd', picked, block_tiles, precision=lax.Precision.HIGHEST)
    return product.reshape(vec_count, NB * B)

def lower_solve(factor, right_side):
    return lax.linalg.triangular_solve(factor, right_side, left_side=True, lower=True)

def one_slice(block_tiles, tile_pattern, slice_item):
    initial, center, halfwidth = slice_item
    previous = initial
    current = (apply_all(initial, block_tiles, tile_pattern) - center * initial) / halfwidth
    for degree in range(DEG - 1):
        following = 2.0 * (apply_all(current, block_tiles, tile_pattern) - center * current) / halfwidth - previous
        previous, current = (current, following)
    gram_matrix = jnp.dot(current, current.T, precision=lax.Precision.HIGHEST)
    factor = jnp.linalg.cholesky(gram_matrix)
    basis_raw = math.sqrt(ORDER) * lower_solve(factor, current)
    imaged = apply_all(basis_raw, block_tiles, tile_pattern)
    projected = jnp.dot(basis_raw, imaged.T, precision=lax.Precision.HIGHEST) / ORDER
    return (basis_raw, projected)

def reference(block_tiles, tile_pattern, start_vectors, centers, halfwidths, dup_pairs):
    basis_raw, projected = lax.map(lambda slice_item: one_slice(block_tiles, tile_pattern, slice_item), (start_vectors, centers, halfwidths))
    columns = jnp.arange(V, dtype=jnp.int32)
    own_index = dup_pairs[:, :, 0]
    their_index = dup_pairs[:, :, 1]
    selector = (their_index[:, :, None] == columns[None, None, :]).astype(jnp.float32)
    target_mask = (own_index[:, :, None] == columns[None, None, :]).astype(jnp.float32)
    lower_basis = jnp.concatenate([jnp.zeros((1, V, ORDER), jnp.float32), basis_raw[:-1]], axis=0)
    lower_rows = jnp.einsum('spv,svn->spn', selector, lower_basis, precision=lax.Precision.HIGHEST)
    correlation = jnp.einsum('spn,svn->spv', lower_rows, basis_raw, precision=lax.Precision.HIGHEST) / ORDER
    filtered_basis = basis_raw - jnp.einsum('spv,spn->svn', target_mask * correlation, lower_rows, precision=lax.Precision.HIGHEST)
    return (filtered_basis, projected)
```

```python
import functools
import math

import jax
import jax.numpy as jnp
from jax import lax
from jax.experimental import pallas as pl
from jax.experimental.pallas import tpu as pltpu
from jax.sharding import PartitionSpec as P

DEG = 8
REACH = 12
F32 = jnp.float32
BF16 = jnp.bfloat16
NN = (((1,), (0,)), ((), ()))
NT = (((1,), (1,)), ((), ()))
TN = (((0,), (0,)), ((), ()))
VMEM = pl.BlockSpec(memory_space=pltpu.VMEM)
SMEM = pl.BlockSpec(memory_space=pltpu.SMEM)
ANY = pl.BlockSpec(memory_space=pl.ANY)
PARAMS = pltpu.CompilerParams(vmem_limit_bytes=40 * 2**20)


def column_of(slot, core, rows):
    pair = 2 * rows
    if slot >= 2 * pair:
        return core * rows + slot - 2 * pair
    chip, block = divmod(slot, pair)
    natural = (block + core * rows) % pair
    return natural - (chip + 1) * pair if core == 0 else natural + (chip + 1) * pair


def sent_slots(rows):
    pair = 2 * rows
    return [s for s in range(5 * rows) if not pair <= s < pair + rows]


def gather_kernel(where, pattern, tiles, sent, table, zeros, sems, *, rows, stored, total):
    pair = 2 * rows
    span = 2 * REACH + pair
    core = where[0] % 2
    first = (where[0] // 2) * pair
    zeros[...] = jnp.zeros_like(zeros)
    for entry in range(rows * span):
        table[entry] = -1
    for row in range(rows):
        for k in range(stored):
            column = pattern[row, k] - first
            column = jnp.where(column >= total // 2, column - total, column)
            column = jnp.where(column < -(total // 2), column + total, column)
            table[row * span + column + REACH] = k
    copies = []
    for place, slot in enumerate(sent_slots(rows)):
        for row in range(rows):
            column = jnp.where(core == 0, column_of(slot, 1, rows), column_of(slot, 0, rows))
            k = table[row * span + column + REACH]
            copies.append((place, row, k))
    for number, (place, row, k) in enumerate(copies):
        target = sent.at[place, row]

        @pl.when(k >= 0)
        def _():
            pltpu.make_async_copy(tiles.at[row, k], target, sems.at[number]).start()

        @pl.when(k < 0)
        def _():
            pltpu.make_async_copy(zeros, target, sems.at[number]).start()

    for number, (place, row, k) in enumerate(copies):
        pltpu.make_async_copy(zeros, sent.at[place, row], sems.at[number]).wait()


def store_tile(tile, high, low, slot, lane):
    tile = tile.T
    top = tile.astype(BF16)
    rest = (tile - top.astype(F32)).astype(BF16)
    width = tile.shape[0]
    high[slot * width : (slot + 1) * width, lane * width : (lane + 1) * width] = top
    low[slot * width : (slot + 1) * width, lane * width : (lane + 1) * width] = rest


def own_weights_kernel(where, table, tiles, high, low, *, rows):
    span = 2 * REACH + 2 * rows
    core = where[0] % 2
    for slot in range(5 * rows):
        for row in range(rows):
            column = jnp.where(core == 0, column_of(slot, 0, rows), column_of(slot, 1, rows))
            k = table[row * span + column + REACH]
            tile = tiles[row, jnp.maximum(k, 0)]
            store_tile(jnp.where(k >= 0, tile, 0.0), high, low, slot, row)


def other_weights_kernel(received, _high, _low, high, low, *, rows):
    places = sent_slots(rows)
    width = received.shape[2]
    for slot in range(5 * rows):
        for row in range(rows):
            if slot in places:
                store_tile(received[places.index(slot), row], high, low, slot, rows + row)
            else:
                blank = jnp.zeros((width, width), BF16)
                lane = rows + row
                high[slot * width : (slot + 1) * width, lane * width : (lane + 1) * width] = blank
                low[slot * width : (slot + 1) * width, lane * width : (lane + 1) * width] = blank


def multiply(vectors, high, low, start, depth):
    count = vectors.shape[0]
    top = vectors.astype(BF16)
    rest = (vectors - top.astype(F32)).astype(BF16)
    both = jnp.concatenate([top, rest], axis=0)
    by_high = lax.dot_general(both, high[start : start + depth, :], NN, preferred_element_type=F32)
    by_low = lax.dot_general(top, low[start : start + depth, :], NN, preferred_element_type=F32)
    return by_high[:count] + (by_high[count:] + by_low)


def own_kernel(vectors, high, low, out, *, start, depth):
    out[...] = multiply(vectors[:, :depth], high, low, start, depth)


def add_kernel(vectors, before, high, low, out, *, start, depth):
    out[...] = before[...] + multiply(vectors[...], high, low, start, depth)


def step_kernel(scale, partial, other, current, previous, out, *, half, first):
    image = partial[:, :half] + other[:, half:], partial[:, half:] + other[:, :half]
    center = scale[0]
    halfwidth = scale[1]
    for number, part in enumerate(image):
        lanes = slice(number * half, (number + 1) * half)
        value = (part - center * current[:, lanes]) / halfwidth
        out[:, lanes] = value if first else 2.0 * value - previous[:, lanes]


def dot(a, b, dims):
    return lax.dot_general(a, b, dims, precision=lax.Precision.HIGHEST, preferred_element_type=F32)


def products_kernel(pair, lower, partial, out, *, half):
    own = pair[:, :half]
    below = lower[...]
    gram = dot(own, own, NT)
    gram_below = dot(below, below, NT)
    mixed = dot(below, own, NT)
    cross = dot(pair[...], partial[...], NT)
    out[...] = jnp.concatenate([gram, gram_below, mixed, cross], axis=1)


def finish_kernel(where, pairs, parts, vectors, lower, filtered, projected, *, order):
    count = vectors.shape[0]
    total = parts[0]
    for device in range(1, parts.shape[0]):
        total = total + parts[device]
    lane = lax.broadcasted_iota(jnp.int32, (count, 4 * count), 1)
    sub = lax.broadcasted_iota(jnp.int32, (count, 4 * count), 0)
    gram = total[:, :count]
    gram_below = total[:, count : 2 * count]
    mixed = total[:, 2 * count : 3 * count]
    cross = total[:, 3 * count :]
    column = lax.broadcasted_iota(jnp.int32, (count, count), 1)
    row = lax.broadcasted_iota(jnp.int32, (count, count), 0)
    eye = (column == row).astype(F32)
    gram_below = jnp.where(where[1] == 0, eye, gram_below)
    work = jnp.concatenate([gram, eye, gram_below, eye], axis=1)
    left = lane < 2 * count
    for k in range(count):
        pivot = jnp.where(left[:1], work[k : k + 1, k : k + 1], work[k : k + 1, 2 * count + k : 2 * count + k + 1])
        root = 1.0 / jnp.sqrt(pivot)
        scaled = work[k : k + 1, :] * root
        factor = jnp.where(left, work[:, k : k + 1], work[:, 2 * count + k : 2 * count + k + 1]) * root
        work = jnp.where(sub > k, work - factor * scaled, jnp.where(sub == k, scaled, work))
    inverse = work[:, count : 2 * count]
    inverse_below = work[:, 3 * count :]
    projected[...] = dot(dot(inverse, cross, NN), inverse, NT)
    correlation = dot(dot(inverse_below, mixed, NN), inverse, NT)
    chosen = jnp.zeros((count, count), F32)
    for p in range(pairs.shape[0]):
        chosen = chosen + ((row == pairs[p, 1]) & (column == pairs[p, 0])).astype(F32)
    removal = dot((chosen * correlation).T, inverse_below, NN)
    filtered[...] = math.sqrt(order) * (dot(inverse, vectors[...], NN) - dot(removal, lower[...], NN))


def call(kernel, out_shape, in_specs, out_specs, **options):
    options.setdefault("compiler_params", PARAMS)
    return pl.pallas_call(kernel, out_shape=out_shape, in_specs=in_specs, out_specs=out_specs, **options)


def local(block_tiles, tile_pattern, start_vectors, centers, halfwidths, dup_pairs):
    rows, stored, width, _ = block_tiles.shape
    devices = lax.axis_size("row")
    cuts = lax.axis_size("cuts")
    chips = devices // 2
    total = rows * devices
    pair = 2 * rows
    half = rows * width
    whole = 2 * half
    initial = start_vectors[0]
    count = initial.shape[0]
    me = lax.axis_index("row")
    where = jnp.stack([me, lax.axis_index("cuts")]).astype(jnp.int32)
    scale = jnp.concatenate([centers, halfwidths])

    swap = [(i, i ^ 1) for i in range(devices)]

    def toward(steps):
        return [(i, (i + (2 * steps if i % 2 == 0 else -2 * steps)) % devices) for i in range(devices)]

    nearer, farther = toward(1), toward(2)
    span = 2 * REACH + pair
    places = len(sent_slots(rows))
    slots = 5 * rows
    weight = jax.ShapeDtypeStruct((slots * width, whole), BF16)
    vec = jax.ShapeDtypeStruct((count, whole), F32)

    sent, table = call(
        functools.partial(gather_kernel, rows=rows, stored=stored, total=total),
        (
            jax.ShapeDtypeStruct((places, rows, width, width), F32),
            jax.ShapeDtypeStruct((rows * span,), jnp.int32),
        ),
        [SMEM, SMEM, ANY],
        (ANY, SMEM),
        scratch_shapes=[pltpu.VMEM((width, width), F32), pltpu.SemaphoreType.DMA((places * rows,))],
    )(where, tile_pattern, block_tiles)
    received = lax.ppermute(sent, "row", swap)
    high, low = call(
        functools.partial(own_weights_kernel, rows=rows), (weight, weight), [SMEM, SMEM, VMEM], (VMEM, VMEM)
    )(where, table, block_tiles)
    high, low = call(
        functools.partial(other_weights_kernel, rows=rows),
        (weight, weight),
        [VMEM, VMEM, VMEM],
        (VMEM, VMEM),
        input_output_aliases={1: 0, 2: 1},
    )(received, high, low)

    def cost(depth):
        return pl.CostEstimate(
            flops=6 * count * depth * whole, bytes_accessed=4 * depth * whole, transcendentals=0
        )

    def part(kernel, start, depth, *vectors):
        return call(
            functools.partial(kernel, start=start * width, depth=depth * width),
            vec,
            [VMEM] * (len(vectors) + 2),
            VMEM,
            cost_estimate=cost(depth * width),
        )(*vectors, high, low)

    def apply_part(vectors):
        near = lax.ppermute(vectors, "row", nearer)
        far = lax.ppermute(vectors, "row", farther)
        partial = part(own_kernel, 2 * pair, rows, vectors)
        partial = part(add_kernel, 0, pair, near, partial)
        return part(add_kernel, pair, pair, far, partial)

    current = jnp.concatenate([initial, lax.ppermute(initial, "row", swap)], axis=1)
    previous = current
    for degree in range(DEG):
        partial = apply_part(current)
        other = lax.ppermute(partial, "row", swap)
        following = call(
            functools.partial(step_kernel, half=half, first=degree == 0),
            vec,
            [SMEM, VMEM, VMEM, VMEM, VMEM],
            VMEM,
        )(scale, partial, other, current, previous)
        previous, current = current, following

    own = current[:, :half]
    lower = lax.ppermute(own, "cuts", [(s, s + 1) for s in range(cuts - 1)])
    partial = apply_part(current)
    products = call(
        functools.partial(products_kernel, half=half),
        jax.ShapeDtypeStruct((count, 4 * count), F32),
        [VMEM, VMEM, VMEM],
        VMEM,
    )(current, lower, partial)
    spread = jnp.broadcast_to(products[None], (devices, *products.shape))
    parts = lax.all_to_all(spread, "row", 0, 0, tiled=True)
    filtered, projected = call(
        functools.partial(finish_kernel, order=total * width),
        (jax.ShapeDtypeStruct((count, half), F32), jax.ShapeDtypeStruct((count, count), F32)),
        [SMEM, SMEM, VMEM, VMEM, VMEM],
        (VMEM, VMEM),
    )(where, dup_pairs[0], parts, own, lower)
    return (filtered[None], projected[None])


def solution(mesh):
    in_specs = (
        P("row", None, None, None),
        P("row", None),
        P("cuts", None, "row"),
        P("cuts"),
        P("cuts"),
        P("cuts", None, None),
    )
    out_specs = (P("cuts", None, "row"), P("cuts", None, None))
    return jax.shard_map(local, mesh=mesh, in_specs=in_specs, out_specs=out_specs, check_vma=False)
```

```python
import functools
import math

import jax
import jax.numpy as jnp
from jax import lax
from jax.experimental import pallas as pl
from jax.experimental.pallas import tpu as pltpu
from jax.sharding import PartitionSpec as P

DEG = 8
REACH = 12
F32 = jnp.float32
BF16 = jnp.bfloat16
NN = (((1,), (0,)), ((), ()))
NT = (((1,), (1,)), ((), ()))
VMEM = pl.BlockSpec(memory_space=pltpu.VMEM)
SMEM = pl.BlockSpec(memory_space=pltpu.SMEM)
HBM = pl.BlockSpec(memory_space=pltpu.HBM)
PARAMS = pltpu.CompilerParams(vmem_limit_bytes=24 * 2**20)


def column_of(slot, core, rows):
    pair = 2 * rows
    if slot >= 2 * pair:
        return core * rows + slot - 2 * pair
    chip, block = divmod(slot, pair)
    natural = (block + core * rows) % pair
    return natural - (chip + 1) * pair if core == 0 else natural + (chip + 1) * pair


def sent_slots(rows):
    pair = 2 * rows
    return [s for s in range(5 * rows) if not pair <= s < pair + rows]


def gather_kernel(where, pattern, tiles, sent, table, zeros, sems, *, rows, stored, total):
    pair = 2 * rows
    span = 2 * REACH + pair
    core = where[0] % 2
    first = (where[0] // 2) * pair
    zeros[...] = jnp.zeros_like(zeros)
    slots = sent_slots(rows)
    for row in range(rows):
        for entry in range(span):
            table[row * span + entry] = -1
        for k in range(stored):
            column = pattern[row, k] - first
            column = jnp.where(column >= total // 2, column - total, column)
            column = jnp.where(column < -(total // 2), column + total, column)
            table[row * span + column + REACH] = k
        for place, slot in enumerate(slots):
            column = jnp.where(core == 0, column_of(slot, 1, rows), column_of(slot, 0, rows))
            k = table[row * span + column + REACH]

            @pl.when(k >= 0)
            def _():
                pltpu.make_async_copy(tiles.at[row, k], sent.at[place, row], sems.at[place, row]).start()

            @pl.when(k < 0)
            def _():
                pltpu.make_async_copy(zeros, sent.at[place, row], sems.at[place, row]).start()

    for row in range(rows):
        for place in range(len(slots)):
            pltpu.make_async_copy(zeros, sent.at[place, row], sems.at[place, row]).wait()


def place_of(slot, rows):
    return divmod(slot, 2 * rows)


def store_tile(tile, high, low, place, lane):
    tile = tile.T
    top = tile.astype(BF16)
    rest = (tile - top.astype(F32)).astype(BF16)
    width = tile.shape[0]
    high[place * width : (place + 1) * width, lane * width : (lane + 1) * width] = top
    low[place * width : (place + 1) * width, lane * width : (lane + 1) * width] = rest


def own_weights_kernel(where, table, tiles, *weights, rows):
    span = 2 * REACH + 2 * rows
    core = where[0] % 2
    for slot in range(5 * rows):
        group, place = place_of(slot, rows)
        for row in range(rows):
            column = jnp.where(core == 0, column_of(slot, 0, rows), column_of(slot, 1, rows))
            k = table[row * span + column + REACH]
            tile = tiles[row, jnp.maximum(k, 0)]
            store_tile(jnp.where(k >= 0, tile, 0.0), *weights[2 * group : 2 * group + 2], place, row)


def other_weights_kernel(received, *refs, rows):
    weights = refs[len(refs) // 2 :]
    places = sent_slots(rows)
    width = received.shape[2]
    for slot in range(5 * rows):
        group, place = place_of(slot, rows)
        for row in range(rows):
            if slot in places:
                tile = received[places.index(slot), row]
            else:
                tile = jnp.zeros((width, width), F32)
            store_tile(tile, *weights[2 * group : 2 * group + 2], place, rows + row)


def multiply(vectors, high, low):
    count = vectors.shape[0]
    top = vectors.astype(BF16)
    rest = (vectors - top.astype(F32)).astype(BF16)
    both = jnp.concatenate([top, rest], axis=0)
    by_high = lax.dot_general(both, high[...], NN, preferred_element_type=F32)
    by_low = lax.dot_general(top, low[...], NN, preferred_element_type=F32)
    return by_high[:count] + (by_high[count:] + by_low)


def own_kernel(vectors, high, low, out):
    out[...] = multiply(vectors[:, : high.shape[0]], high, low)


def add_kernel(vectors, before, high, low, out):
    out[...] = before[...] + multiply(vectors[...], high, low)


def join_kernel(first, second, out, *, half):
    out[:, :half] = first[...]
    out[:, half:] = second[...]


def step_kernel(factors, partial, other, current, previous, out, *, half, first):
    image = partial[:, :half] + other[:, half:], partial[:, half:] + other[:, :half]
    scale = factors[0:1, 0:1]
    shift = factors[1:2, 0:1]
    for number, part in enumerate(image):
        lanes = slice(number * half, (number + 1) * half)
        value = scale * part - shift * current[:, lanes]
        out[:, lanes] = value if first else 2.0 * value - previous[:, lanes]


def dot(a, b, dims):
    return lax.dot_general(a, b, dims, precision=lax.Precision.HIGHEST, preferred_element_type=F32)


def pack(square):
    count = square.shape[0]
    strip = count * count // 128
    return jnp.concatenate([square[i * strip : (i + 1) * strip] for i in range(count // strip)], axis=1)


def unpack(rows, count):
    return jnp.concatenate([rows[:, i : i + count] for i in range(0, 128, count)], axis=0)


def gram_kernel(where, pairs, pair, lower, packed, chosen, *, half):
    own = pair[:, :half]
    below = lower[...]
    squares = [dot(own, own, NT), dot(below, below, NT), dot(below, own, NT)]
    packed[...] = jnp.concatenate([pack(square) for square in squares], axis=0)
    row = lax.broadcasted_iota(jnp.int32, chosen.shape, 0)
    column = lax.broadcasted_iota(jnp.int32, chosen.shape, 1)
    total = jnp.zeros(chosen.shape, F32)
    for p in range(pairs.shape[1]):
        total = total + ((row == pairs[1, p]) & (column == pairs[0, p])).astype(F32)
    chosen[...] = jnp.where(where[1] == 0, 0.0, total)


def cross_kernel(pair, partial, packed, out):
    every = jnp.concatenate([packed[...], pack(dot(pair[...], partial[...], NT))], axis=0)
    for device in range(out.shape[0]):
        out[device] = every


def summed(parts):
    total = parts[0]
    for device in range(1, parts.shape[0]):
        total = total + parts[device]
    return total


def inverses(gram, gram_below):
    count = gram.shape[0]
    block = 8
    row = lax.broadcasted_iota(jnp.int32, (count, count), 0)
    column = lax.broadcasted_iota(jnp.int32, (count, count), 1)
    eye = (row == column).astype(F32)
    work = jnp.concatenate([gram, eye, gram_below, eye], axis=1)
    sub = lax.broadcasted_iota(jnp.int32, work.shape, 0)
    left = lax.broadcasted_iota(jnp.int32, work.shape, 1) < 2 * count

    def spread(values, k):
        return jnp.where(left[: values.shape[0]], values[:, k : k + 1], values[:, 2 * count + k : 2 * count + k + 1])

    for k in range(0, count, block):
        rows = [work[k + i : k + i + 1, :] for i in range(block)]
        corner = [[spread(r, k + j) for j in range(block)] for r in rows]
        columns = [spread(work, k + j) for j in range(block)]
        for i in range(block):
            pivot = 1.0 / corner[i][i]
            factor = jnp.where(sub > k + i, columns[i] * pivot, 0.0)
            work = work - factor * rows[i]
            for j in range(i + 1, block):
                columns[j] = columns[j] - factor * corner[i][j]
                ratio = corner[j][i] * pivot
                rows[j] = rows[j] - ratio * rows[i]
                for m in range(i + 1, block):
                    corner[j][m] = corner[j][m] - ratio * corner[i][m]

    def scaled(start):
        pivots = jnp.sum(eye * work[:, start : start + count], axis=1, keepdims=True)
        return work[:, start + count : start + 2 * count] * (1.0 / jnp.sqrt(pivots))

    return scaled(0), scaled(2 * count)


def finish_kernel(parts, chosen, vectors, lower, filtered, projected, *, order):
    count = vectors.shape[0]
    total = summed(parts)
    strip = count * count // 128
    gram, gram_below, mixed, cross = (unpack(total[i * strip : (i + 1) * strip], count) for i in range(4))
    inverse, inverse_below = inverses(gram, gram_below)
    correlation = dot(dot(inverse_below, mixed, NN), inverse, NT)
    projected[...] = dot(dot(inverse, cross, NN), inverse, NT)
    some = jnp.max(chosen[...]) > 0.0
    removal = jnp.where(some, dot((chosen[...] * correlation).T, inverse_below, NN), 0.0)
    filtered[...] = math.sqrt(order) * (dot(inverse, vectors[...], NN) - dot(removal, lower[...], NN))


def call(kernel, out_shape, in_specs, out_specs, **options):
    options.setdefault("compiler_params", PARAMS)
    options.setdefault("cost_estimate", pl.CostEstimate(flops=10**6, bytes_accessed=10**5, transcendentals=0))
    return pl.pallas_call(kernel, out_shape=out_shape, in_specs=in_specs, out_specs=out_specs, **options)


def local(block_tiles, tile_pattern, start_vectors, centers, halfwidths, dup_pairs):
    rows, stored, width, _ = block_tiles.shape
    devices = lax.axis_size("row")
    cuts = lax.axis_size("cuts")
    chips = devices // 2
    total = rows * devices
    pair = 2 * rows
    half = rows * width
    whole = 2 * half
    initial = start_vectors[0]
    count = initial.shape[0]
    me = lax.axis_index("row")
    where = jnp.stack([me, lax.axis_index("cuts")]).astype(jnp.int32)
    factors = jnp.broadcast_to(jnp.concatenate([1.0 / halfwidths, centers / halfwidths])[:, None], (2, 128))

    swap = [(i, i ^ 1) for i in range(devices)]
    below = [(s, (s + 1) % cuts) for s in range(cuts)]

    def toward(steps):
        return [(i, (i + (2 * steps if i % 2 == 0 else -2 * steps)) % devices) for i in range(devices)]

    nearer, farther = toward(1), toward(2)
    span = 2 * REACH + pair
    places = len(sent_slots(rows))
    shapes = tuple(
        jax.ShapeDtypeStruct((depth * width, whole), BF16) for depth in (pair, pair, rows) for _ in range(2)
    )
    vec = jax.ShapeDtypeStruct((count, whole), F32)

    beside = lax.ppermute(initial, "row", swap)
    sent, table = call(
        functools.partial(gather_kernel, rows=rows, stored=stored, total=total),
        (
            jax.ShapeDtypeStruct((places, rows, width, width), F32),
            jax.ShapeDtypeStruct((rows * span,), jnp.int32),
        ),
        [SMEM, SMEM, HBM],
        (VMEM, SMEM),
        scratch_shapes=[pltpu.VMEM((width, width), F32), pltpu.SemaphoreType.DMA((places, rows))],
    )(where, tile_pattern, pltpu.with_memory_space_constraint(block_tiles, pltpu.HBM))
    sent, beside = lax.optimization_barrier((sent, beside))
    received = lax.ppermute(sent, "row", swap)
    weights = call(
        functools.partial(own_weights_kernel, rows=rows), shapes, [SMEM, SMEM, VMEM], (VMEM,) * 6
    )(where, table, block_tiles)
    weights = call(
        functools.partial(other_weights_kernel, rows=rows),
        shapes,
        [VMEM] * 7,
        (VMEM,) * 6,
        input_output_aliases={1 + i: i for i in range(6)},
    )(received, *weights)
    near_weights, far_weights, own_weights = weights[:2], weights[2:4], weights[4:]

    def part(kernel, group, *vectors):
        high, low = group
        depth = high.shape[0]
        return call(
            kernel,
            vec,
            [VMEM] * (len(vectors) + 2),
            VMEM,
            cost_estimate=pl.CostEstimate(
                flops=6 * count * depth * whole, bytes_accessed=4 * depth * whole, transcendentals=0
            ),
        )(*vectors, high, low)

    def apply_part(vectors):
        near = lax.ppermute(vectors, "row", nearer)
        far = lax.ppermute(vectors, "row", farther)
        partial = part(own_kernel, own_weights, vectors)
        partial = part(add_kernel, far_weights, far, partial)
        return part(add_kernel, near_weights, near, partial)

    current = call(functools.partial(join_kernel, half=half), vec, [VMEM, VMEM], VMEM)(initial, beside)
    previous = current
    for degree in range(DEG):
        partial = apply_part(current)
        other = lax.ppermute(partial, "row", swap)
        following = call(
            functools.partial(step_kernel, half=half, first=degree == 0),
            vec,
            [VMEM] * 5,
            VMEM,
        )(factors, partial, other, current, previous)
        previous, current = current, following

    own = current[:, :half]
    strip = count * count // 128
    lower = lax.ppermute(own, "cuts", below)
    partial = apply_part(current)
    small = jax.ShapeDtypeStruct((count, count), F32)
    lower, partial = lax.optimization_barrier((lower, partial))
    packed, chosen = call(
        functools.partial(gram_kernel, half=half),
        (jax.ShapeDtypeStruct((3 * strip, 128), F32), small),
        [SMEM, SMEM, VMEM, VMEM],
        (VMEM, VMEM),
    )(where, dup_pairs[0].T, current, lower)
    products = call(
        cross_kernel, jax.ShapeDtypeStruct((devices, 4 * strip, 128), F32), [VMEM, VMEM, VMEM], VMEM
    )(current, partial, packed)
    parts = lax.all_to_all(products, "row", 0, 0, tiled=True)
    filtered, projected = call(
        functools.partial(finish_kernel, order=total * width),
        (jax.ShapeDtypeStruct((count, half), F32), small),
        [VMEM] * 4,
        (VMEM, VMEM),
    )(parts, chosen, own, lower)
    return (filtered[None], projected[None])


def solution(mesh):
    in_specs = (
        P("row", None, None, None),
        P("row", None),
        P("cuts", None, "row"),
        P("cuts"),
        P("cuts"),
        P("cuts", None, None),
    )
    out_specs = (P("cuts", None, "row"), P("cuts", None, None))
    return jax.shard_map(local, mesh=mesh, in_specs=in_specs, out_specs=out_specs, check_vma=False)
```

```python
import functools
import math

import jax
import jax.numpy as jnp
from jax import lax
from jax.experimental import pallas as pl
from jax.experimental.pallas import tpu as pltpu
from jax.sharding import PartitionSpec as P

DEG = 8
REACH = 12
F32 = jnp.float32
BF16 = jnp.bfloat16
NN = (((1,), (0,)), ((), ()))
NT = (((1,), (1,)), ((), ()))
VMEM = pl.BlockSpec(memory_space=pltpu.VMEM)
SMEM = pl.BlockSpec(memory_space=pltpu.SMEM)
HBM = pl.BlockSpec(memory_space=pltpu.HBM)
PARAMS = pltpu.CompilerParams(vmem_limit_bytes=24 * 2**20)


def column_of(slot, core, rows):
    pair = 2 * rows
    if slot >= 2 * pair:
        return core * rows + slot - 2 * pair
    chip, block = divmod(slot, pair)
    natural = (block + core * rows) % pair
    return natural - (chip + 1) * pair if core == 0 else natural + (chip + 1) * pair


def sent_slots(rows):
    pair = 2 * rows
    return [s for s in range(5 * rows) if not pair <= s < pair + rows]


def offset_in_span(block, start, total):
    offset = block - start
    offset = jnp.where(offset < 0, offset + total, offset)
    return jnp.where(offset >= total, offset - total, offset)


def gather_kernel(pattern, tiles, sent, blocks, places, count, sems, *, rows, stored, total):
    pair = 2 * rows
    span = 2 * REACH + pair
    copy = pltpu.make_async_copy(pattern, blocks, sems.at[0])
    copy.start()
    me = lax.axis_index("row")
    core = me % 2
    start = (me // 2) * pair - REACH
    for offset in range(span):
        places[offset] = -1
    for place, slot in enumerate(sent_slots(rows)):
        column = jnp.where(core == 0, column_of(slot, 1, rows), column_of(slot, 0, rows))
        places[column + REACH] = place
    count[0] = 0
    sent[...] = jnp.zeros_like(sent)
    copy.wait()
    for row in range(rows):
        for k in range(stored):
            place = places[offset_in_span(blocks[row, k], start, total)]

            @pl.when(place >= 0)
            def _():
                count[0] += 1
                pltpu.make_async_copy(tiles.at[row, k], sent.at[place, row], sems.at[1]).start()

    @pl.loop(0, count[0])
    def _(_):
        pltpu.make_async_copy(tiles.at[0, 0], sent.at[0, 0], sems.at[1]).wait()


def place_of(slot, rows):
    return divmod(slot, 2 * rows)


def store_tile(tile, high, low, place, lane):
    tile = tile.T
    top = tile.astype(BF16)
    rest = (tile - top.astype(F32)).astype(BF16)
    width = tile.shape[0]
    high[place * width : (place + 1) * width, lane * width : (lane + 1) * width] = top
    low[place * width : (place + 1) * width, lane * width : (lane + 1) * width] = rest


def own_weights_kernel(pattern, tiles, *refs, rows, stored, total):
    weights, (blocks, table, sem) = refs[:6], refs[6:]
    copy = pltpu.make_async_copy(pattern, blocks, sem)
    copy.start()
    span = 2 * REACH + 2 * rows
    me = lax.axis_index("row")
    core = me % 2
    start = (me // 2) * 2 * rows - REACH
    for entry in range(rows * span):
        table[entry] = -1
    copy.wait()
    for row in range(rows):
        for k in range(stored):
            table[row * span + offset_in_span(blocks[row, k], start, total)] = k
    for slot in range(5 * rows):
        group, place = place_of(slot, rows)
        for row in range(rows):
            column = jnp.where(core == 0, column_of(slot, 0, rows), column_of(slot, 1, rows))
            k = table[row * span + column + REACH]
            tile = tiles[row, jnp.maximum(k, 0)]
            store_tile(jnp.where(k >= 0, tile, 0.0), *weights[2 * group : 2 * group + 2], place, row)


def other_weights_kernel(received, *refs, rows):
    weights = refs[len(refs) // 2 :]
    places = sent_slots(rows)
    width = received.shape[2]
    for slot in range(5 * rows):
        group, place = place_of(slot, rows)
        for row in range(rows):
            if slot in places:
                tile = received[places.index(slot), row]
            else:
                tile = jnp.zeros((width, width), F32)
            store_tile(tile, *weights[2 * group : 2 * group + 2], place, rows + row)


def multiply(vectors, high, low):
    count = vectors.shape[0]
    top = vectors.astype(BF16)
    rest = (vectors - top.astype(F32)).astype(BF16)
    both = jnp.concatenate([top, rest], axis=0)
    by_high = lax.dot_general(both, high[...], NN, preferred_element_type=F32)
    by_low = lax.dot_general(top, low[...], NN, preferred_element_type=F32)
    return by_high[:count] + (by_high[count:] + by_low)


def own_kernel(vectors, high, low, out):
    out[...] = multiply(vectors[:, : high.shape[0]], high, low)


def add_kernel(vectors, before, high, low, out):
    out[...] = before[...] + multiply(vectors[...], high, low)


def join_kernel(first, second, out, *, half):
    out[:, :half] = first[...]
    out[:, half:] = second[...]


def halves(partial, other, half):
    yield slice(0, half), partial[:, :half] + other[:, half:]
    yield slice(half, 2 * half), partial[:, half:] + other[:, :half]


def image_kernel(partial, other, out, *, half):
    for lanes, image in halves(partial, other, half):
        out[:, lanes] = image


def second_kernel(factors, partial, other, image, initial, first, second, *, half):
    scale = factors[0:1, 0:1]
    shift = factors[1:2, 0:1]
    for lanes, twice in halves(partial, other, half):
        once = image[:, lanes]
        start = initial[:, lanes]
        value = scale * once - shift * start
        first[:, lanes] = value
        second[:, lanes] = 2.0 * (scale * (scale * twice - shift * once) - shift * value) - start


def step_kernel(factors, partial, other, current, previous, out, *, half):
    scale = factors[0:1, 0:1]
    shift = factors[1:2, 0:1]
    for lanes, image in halves(partial, other, half):
        out[:, lanes] = 2.0 * (scale * image - shift * current[:, lanes]) - previous[:, lanes]


def dot(a, b, dims):
    return lax.dot_general(a, b, dims, precision=lax.Precision.HIGHEST, preferred_element_type=F32)


def pack(square):
    count = square.shape[0]
    strip = count * count // 128
    return jnp.concatenate([square[i * strip : (i + 1) * strip] for i in range(count // strip)], axis=1)


def unpack(rows, count):
    return jnp.concatenate([rows[:, i : i + count] for i in range(0, 128, count)], axis=0)


def gram_kernel(pairs, pair, lower, packed, chosen, *, half):
    own = pair[:, :half]
    below = lower[...]
    squares = [dot(own, own, NT), dot(below, below, NT), dot(below, own, NT)]
    packed[...] = jnp.concatenate([pack(square) for square in squares], axis=0)
    row = lax.broadcasted_iota(jnp.int32, chosen.shape, 0)
    column = lax.broadcasted_iota(jnp.int32, chosen.shape, 1)
    total = jnp.zeros(chosen.shape, F32)
    for p in range(pairs.shape[1]):
        total = total + ((row == pairs[1, p]) & (column == pairs[0, p])).astype(F32)
    chosen[...] = jnp.where(lax.axis_index("cuts") == 0, 0.0, total)


def cross_kernel(pair, partial, packed, out):
    out[...] = jnp.concatenate([packed[...], pack(dot(pair[...], partial[...], NT))], axis=0)


def spread_kernel(one, other, out):
    both = one[...] + other[...]
    for chip in range(out.shape[0]):
        out[chip] = both


def summed(parts):
    total = parts[0]
    for device in range(1, parts.shape[0]):
        total = total + parts[device]
    return total


def inverses(gram, gram_below):
    count = gram.shape[0]
    block = 8
    row = lax.broadcasted_iota(jnp.int32, (count, count), 0)
    column = lax.broadcasted_iota(jnp.int32, (count, count), 1)
    eye = (row == column).astype(F32)
    work = jnp.concatenate([gram, eye, gram_below, eye], axis=1)
    sub = lax.broadcasted_iota(jnp.int32, work.shape, 0)
    left = lax.broadcasted_iota(jnp.int32, work.shape, 1) < 2 * count

    def spread(values, k):
        return jnp.where(left[: values.shape[0]], values[:, k : k + 1], values[:, 2 * count + k : 2 * count + k + 1])

    for k in range(0, count, block):
        rows = [work[k + i : k + i + 1, :] for i in range(block)]
        corner = [[spread(r, k + j) for j in range(block)] for r in rows]
        columns = [spread(work, k + j) for j in range(block)]
        for i in range(block):
            pivot = 1.0 / corner[i][i]
            factor = jnp.where(sub > k + i, columns[i] * pivot, 0.0)
            work = work - factor * rows[i]
            for j in range(i + 1, block):
                columns[j] = columns[j] - factor * corner[i][j]
                ratio = corner[j][i] * pivot
                rows[j] = rows[j] - ratio * rows[i]
                for m in range(i + 1, block):
                    corner[j][m] = corner[j][m] - ratio * corner[i][m]

    def scaled(start):
        pivots = jnp.sum(eye * work[:, start : start + count], axis=1, keepdims=True)
        return work[:, start + count : start + 2 * count] * (1.0 / jnp.sqrt(pivots))

    return scaled(0), scaled(2 * count)


def finish_kernel(parts, chosen, vectors, lower, filtered, projected, *, order):
    count = vectors.shape[0]
    total = summed(parts)
    strip = count * count // 128
    gram, gram_below, mixed, cross = (unpack(total[i * strip : (i + 1) * strip], count) for i in range(4))
    inverse, inverse_below = inverses(gram, gram_below)
    correlation = dot(dot(inverse_below, mixed, NN), inverse, NT)
    projected[...] = dot(dot(inverse, cross, NN), inverse, NT)
    some = jnp.max(chosen[...]) > 0.0
    removal = jnp.where(some, dot((chosen[...] * correlation).T, inverse_below, NN), 0.0)
    filtered[...] = math.sqrt(order) * (dot(inverse, vectors[...], NN) - dot(removal, lower[...], NN))


def call(kernel, out_shape, in_specs, out_specs, **options):
    options.setdefault("compiler_params", PARAMS)
    options.setdefault("cost_estimate", pl.CostEstimate(flops=10**6, bytes_accessed=10**5, transcendentals=0))
    return pl.pallas_call(kernel, out_shape=out_shape, in_specs=in_specs, out_specs=out_specs, **options)


def local(block_tiles, tile_pattern, start_vectors, centers, halfwidths, dup_pairs):
    rows, stored, width, _ = block_tiles.shape
    devices = lax.axis_size("row")
    cuts = lax.axis_size("cuts")
    chips = devices // 2
    total = rows * devices
    pair = 2 * rows
    half = rows * width
    whole = 2 * half
    initial = start_vectors[0]
    count = initial.shape[0]

    swap = [(i, i ^ 1) for i in range(devices)]
    below = [(s, (s + 1) % cuts) for s in range(cuts)]

    def toward(steps):
        return [(i, (i + (2 * steps if i % 2 == 0 else -2 * steps)) % devices) for i in range(devices)]

    nearer, farther = toward(1), toward(2)
    span = 2 * REACH + pair
    places = len(sent_slots(rows))
    shapes = tuple(
        jax.ShapeDtypeStruct((depth * width, whole), BF16) for depth in (pair, pair, rows) for _ in range(2)
    )
    vec = jax.ShapeDtypeStruct((count, whole), F32)

    beside = lax.ppermute(initial, "row", swap)
    sent = call(
        functools.partial(gather_kernel, rows=rows, stored=stored, total=total),
        jax.ShapeDtypeStruct((places, rows, width, width), F32),
        [HBM, HBM],
        VMEM,
        scratch_shapes=[
            pltpu.SMEM((rows, stored), jnp.int32),
            pltpu.SMEM((span,), jnp.int32),
            pltpu.SMEM((1,), jnp.int32),
            pltpu.SemaphoreType.DMA((2,)),
        ],
        cost_estimate=pl.CostEstimate(flops=0, bytes_accessed=8 * 10**6, transcendentals=0),
    )(*(pltpu.with_memory_space_constraint(array, pltpu.HBM) for array in (tile_pattern, block_tiles)))
    sent, beside = lax.optimization_barrier((sent, beside))
    received = lax.ppermute(sent, "row", swap)
    weights = call(
        functools.partial(own_weights_kernel, rows=rows, stored=stored, total=total),
        shapes,
        [HBM, VMEM],
        (VMEM,) * 6,
        scratch_shapes=[
            pltpu.SMEM((rows, stored), jnp.int32),
            pltpu.SMEM((rows * span,), jnp.int32),
            pltpu.SemaphoreType.DMA,
        ],
    )(pltpu.with_memory_space_constraint(tile_pattern, pltpu.HBM), block_tiles)
    weights = call(
        functools.partial(other_weights_kernel, rows=rows),
        shapes,
        [VMEM] * 7,
        (VMEM,) * 6,
        input_output_aliases={1 + i: i for i in range(6)},
    )(received, *weights)
    near_weights, far_weights, own_weights = weights[:2], weights[2:4], weights[4:]

    def part(kernel, group, *vectors):
        high, low = group
        depth = high.shape[0]
        return call(
            kernel,
            vec,
            [VMEM] * (len(vectors) + 2),
            VMEM,
            cost_estimate=pl.CostEstimate(
                flops=6 * count * depth * whole, bytes_accessed=4 * depth * whole, transcendentals=0
            ),
        )(*vectors, high, low)

    def apply_part(vectors):
        near = lax.ppermute(vectors, "row", nearer)
        far = lax.ppermute(vectors, "row", farther)
        partial = part(own_kernel, own_weights, vectors)
        partial = part(add_kernel, far_weights, far, partial)
        return part(add_kernel, near_weights, near, partial)

    current = call(functools.partial(join_kernel, half=half), vec, [VMEM, VMEM], VMEM)(initial, beside)
    def images(vectors):
        partial = apply_part(vectors)
        return partial, lax.ppermute(partial, "row", swap)

    def step(kernel, out_shape, *operands):
        out_specs = VMEM if out_shape is vec else (VMEM,) * len(out_shape)
        return call(functools.partial(kernel, half=half), out_shape, [VMEM] * len(operands), out_specs)(*operands)

    factors = jnp.broadcast_to(jnp.concatenate([1.0 / halfwidths, centers / halfwidths])[:, None], (2, 128))
    image = step(image_kernel, vec, *images(current))
    previous, current = step(second_kernel, (vec, vec), factors, *images(image), image, current)
    for _ in range(DEG - 2):
        previous, current = current, step(step_kernel, vec, factors, *images(current), current, previous)

    own = current[:, :half]
    strip = count * count // 128
    lower = lax.ppermute(own, "cuts", below)
    partial = apply_part(current)
    small = jax.ShapeDtypeStruct((count, count), F32)
    lower, partial = lax.optimization_barrier((lower, partial))
    packed, chosen = call(
        functools.partial(gram_kernel, half=half),
        (jax.ShapeDtypeStruct((3 * strip, 128), F32), small),
        [SMEM, VMEM, VMEM],
        (VMEM, VMEM),
    )(dup_pairs[0].T, current, lower)
    sums = jax.ShapeDtypeStruct((4 * strip, 128), F32)
    products = call(cross_kernel, sums, [VMEM, VMEM, VMEM], VMEM)(current, partial, packed)
    beside = lax.ppermute(products, "row", swap)
    spread = call(spread_kernel, jax.ShapeDtypeStruct((chips, *sums.shape), F32), [VMEM, VMEM], VMEM)(products, beside)
    same_core = [[2 * chip + core for chip in range(chips)] for core in range(2)]
    parts = lax.all_to_all(spread, "row", 0, 0, tiled=True, axis_index_groups=same_core)
    filtered, projected = call(
        functools.partial(finish_kernel, order=total * width),
        (jax.ShapeDtypeStruct((count, half), F32), small),
        [VMEM] * 4,
        (VMEM, VMEM),
    )(parts, chosen, own, lower)
    return (filtered[None], projected[None])


def solution(mesh):
    in_specs = (
        P("row", None, None, None),
        P("row", None),
        P("cuts", None, "row"),
        P("cuts"),
        P("cuts"),
        P("cuts", None, None),
    )
    out_specs = (P("cuts", None, "row"), P("cuts", None, None))
    return jax.shard_map(local, mesh=mesh, in_specs=in_specs, out_specs=out_specs, check_vma=False)
```

```python
import functools
import math

import jax
import jax.numpy as jnp
from jax import lax
from jax.experimental import pallas as pl
from jax.experimental.pallas import tpu as pltpu
from jax.sharding import PartitionSpec as P

DEG = 8
REACH = 12
F32 = jnp.float32
BF16 = jnp.bfloat16
NN = (((1,), (0,)), ((), ()))
NT = (((1,), (1,)), ((), ()))
VMEM = pl.BlockSpec(memory_space=pltpu.VMEM)
SMEM = pl.BlockSpec(memory_space=pltpu.SMEM)
HBM = pl.BlockSpec(memory_space=pltpu.HBM)
PARAMS = pltpu.CompilerParams(vmem_limit_bytes=24 * 2**20)


def column_of(slot, core, rows):
    pair = 2 * rows
    if slot >= 2 * pair:
        return core * rows + slot - 2 * pair
    chip, block = divmod(slot, pair)
    natural = (block + core * rows) % pair
    return natural - (chip + 1) * pair if core == 0 else natural + (chip + 1) * pair


def sent_slots(rows):
    pair = 2 * rows
    return [s for s in range(5 * rows) if not pair <= s < pair + rows]


def offset_in_span(block, start, total):
    offset = block - start
    offset = jnp.where(offset < 0, offset + total, offset)
    return jnp.where(offset >= total, offset - total, offset)


def gather_kernel(pattern, tiles, sent, blocks, places, count, sems, *, rows, stored, total):
    pair = 2 * rows
    span = 2 * REACH + pair
    copy = pltpu.make_async_copy(pattern, blocks, sems.at[0])
    copy.start()
    me = lax.axis_index("row")
    core = me % 2
    start = (me // 2) * pair - REACH
    for offset in range(span):
        places[offset] = -1
    for place, slot in enumerate(sent_slots(rows)):
        column = jnp.where(core == 0, column_of(slot, 1, rows), column_of(slot, 0, rows))
        places[column + REACH] = place
    count[0] = 0
    sent[...] = jnp.zeros_like(sent)
    copy.wait()
    for row in range(rows):
        for k in range(stored):
            place = places[offset_in_span(blocks[row, k], start, total)]

            @pl.when(place >= 0)
            def _():
                count[0] += 1
                pltpu.make_async_copy(tiles.at[row, k], sent.at[place, row], sems.at[1]).start()

    @pl.loop(0, count[0])
    def _(_):
        pltpu.make_async_copy(tiles.at[0, 0], sent.at[0, 0], sems.at[1]).wait()


def place_of(slot, rows):
    return divmod(slot, 2 * rows)


def store_tile(tile, high, low, place, lane):
    tile = tile.T
    top = tile.astype(BF16)
    rest = (tile - top.astype(F32)).astype(BF16)
    width = tile.shape[0]
    high[place * width : (place + 1) * width, lane * width : (lane + 1) * width] = top
    low[place * width : (place + 1) * width, lane * width : (lane + 1) * width] = rest


def own_weights_kernel(pattern, tiles, *refs, rows, stored, total):
    weights, (blocks, table, sem) = refs[:6], refs[6:]
    copy = pltpu.make_async_copy(pattern, blocks, sem)
    copy.start()
    span = 2 * REACH + 2 * rows
    me = lax.axis_index("row")
    core = me % 2
    start = (me // 2) * 2 * rows - REACH
    for entry in range(rows * span):
        table[entry] = -1
    copy.wait()
    for row in range(rows):
        for k in range(stored):
            table[row * span + offset_in_span(blocks[row, k], start, total)] = k
    for slot in range(5 * rows):
        group, place = place_of(slot, rows)
        for row in range(rows):
            column = jnp.where(core == 0, column_of(slot, 0, rows), column_of(slot, 1, rows))
            k = table[row * span + column + REACH]
            tile = tiles[row, jnp.maximum(k, 0)]
            store_tile(jnp.where(k >= 0, tile, 0.0), *weights[2 * group : 2 * group + 2], place, row)


def other_weights_kernel(received, *refs, rows):
    weights = refs[len(refs) // 2 :]
    places = sent_slots(rows)
    width = received.shape[2]
    for slot in range(5 * rows):
        group, place = place_of(slot, rows)
        for row in range(rows):
            if slot in places:
                tile = received[places.index(slot), row]
            else:
                tile = jnp.zeros((width, width), F32)
            store_tile(tile, *weights[2 * group : 2 * group + 2], place, rows + row)


def multiply(vectors, high, low):
    count = vectors.shape[0]
    top = vectors.astype(BF16)
    rest = (vectors - top.astype(F32)).astype(BF16)
    both = jnp.concatenate([top, rest], axis=0)
    by_high = lax.dot_general(both, high[...], NN, preferred_element_type=F32)
    by_low = lax.dot_general(top, low[...], NN, preferred_element_type=F32)
    return by_high[:count] + (by_high[count:] + by_low)


def own_kernel(vectors, _after, high, low, out):
    out[...] = multiply(vectors[:, : high.shape[0]], high, low)


def add_kernel(vectors, before, high, low, out):
    out[...] = before[...] + multiply(vectors[...], high, low)


def join_kernel(first, second, out, *, half):
    out[:, :half] = first[...]
    out[:, half:] = second[...]


def halves(partial, other, half):
    yield slice(0, half), partial[:, :half] + other[:, half:]
    yield slice(half, 2 * half), partial[:, half:] + other[:, :half]


def image_kernel(partial, other, out, *, half):
    for lanes, image in halves(partial, other, half):
        out[:, lanes] = image


def second_kernel(factors, partial, other, image, initial, first, second, *, half):
    scale = factors[0:1, 0:1]
    shift = factors[1:2, 0:1]
    for lanes, twice in halves(partial, other, half):
        once = image[:, lanes]
        start = initial[:, lanes]
        value = scale * once - shift * start
        first[:, lanes] = value
        second[:, lanes] = 2.0 * (scale * (scale * twice - shift * once) - shift * value) - start


def step_kernel(factors, partial, other, current, previous, out, *, half):
    scale = factors[0:1, 0:1]
    shift = factors[1:2, 0:1]
    for lanes, image in halves(partial, other, half):
        out[:, lanes] = 2.0 * (scale * image - shift * current[:, lanes]) - previous[:, lanes]


def dot(a, b, dims):
    return lax.dot_general(a, b, dims, precision=lax.Precision.HIGHEST, preferred_element_type=F32)


def chosen_kernel(pairs, _after, out):
    row = lax.broadcasted_iota(jnp.int32, out.shape, 0)
    column = lax.broadcasted_iota(jnp.int32, out.shape, 1)
    total = jnp.zeros(out.shape, F32)
    for p in range(pairs.shape[1]):
        total = total + ((row == pairs[0, p]) & (column == pairs[1, p])).astype(F32)
    out[...] = jnp.where(lax.axis_index("cuts") == 0, 0.0, total)


def gram_kernel(pair, lower, gram, below, mixed, *, half):
    own = pair[:, :half]
    gram[...] = dot(own, own, NT)
    below[...] = dot(lower[...], lower[...], NT)
    mixed[...] = dot(own, lower[...], NT)


def cross_kernel(pair, partial, gram, below, mixed, out):
    cross = dot(pair[...], partial[...], NT)
    out[...] = jnp.concatenate([gram[...], mixed[...], below[...], cross], axis=1)


def spread_kernel(one, other, out):
    both = one[...] + other[...]
    for chip in range(out.shape[0]):
        out[chip] = both


def summed(parts):
    total = parts[0]
    for device in range(1, parts.shape[0]):
        total = total + parts[device]
    return total


def inverses(squares):
    count = squares.shape[0]
    block = 16
    sub = lax.broadcasted_iota(jnp.int32, squares.shape, 0)
    lane = lax.broadcasted_iota(jnp.int32, squares.shape, 1)
    left = lane < 2 * count
    place = jnp.where(left, lane, lane - 2 * count)
    work = jnp.where(place < count, squares, (place == sub + count).astype(F32))
    for k in range(0, count, block):
        columns = [
            jnp.where(left, work[:, m : m + 1], work[:, 2 * count + m : 2 * count + m + 1]) for m in range(k, k + block)
        ]
        for i in range(block):
            here = slice(k + i, k + i + 1)
            factor = jnp.where(sub > k + i, columns[i] * (1.0 / columns[i][here]), 0.0)
            for j in range(i + 1, block):
                columns[j] = columns[j] - factor * columns[j][here]
            work = work - factor * work[here]
    pivots = jnp.where(place == sub, work, 0.0)
    for start in (0, 2 * count):
        pivot = jnp.sum(pivots[:, start : start + count], axis=1, keepdims=True)
        yield work[:, start + count : start + 2 * count] * (1.0 / jnp.sqrt(pivot))


def finish_kernel(parts, chosen, vectors, lower, filtered, projected, *, order):
    count = vectors.shape[0]
    total = summed(parts)
    mixed, cross = total[:, count : 2 * count], total[:, 3 * count :]
    inverse, inverse_below = inverses(total)
    scale = math.sqrt(order)
    basis = scale * dot(inverse, vectors[...], NN)
    lower_basis = scale * dot(inverse_below, lower[...], NN)
    correlation = dot(dot(inverse, mixed, NN), inverse_below, NT)
    projected[...] = dot(dot(inverse, cross, NN), inverse, NT)
    some = jnp.max(chosen[...]) > 0.0
    removal = jnp.where(some, dot(chosen[...] * correlation, lower_basis, NN), 0.0)
    filtered[...] = basis - removal


def call(kernel, out_shape, in_specs, out_specs, **options):
    options.setdefault("compiler_params", PARAMS)
    options.setdefault("cost_estimate", pl.CostEstimate(flops=10**6, bytes_accessed=10**5, transcendentals=0))
    return pl.pallas_call(kernel, out_shape=out_shape, in_specs=in_specs, out_specs=out_specs, **options)


def local(block_tiles, tile_pattern, start_vectors, centers, halfwidths, dup_pairs):
    rows, stored, width, _ = block_tiles.shape
    devices = lax.axis_size("row")
    cuts = lax.axis_size("cuts")
    chips = devices // 2
    total = rows * devices
    pair = 2 * rows
    half = rows * width
    whole = 2 * half
    initial = start_vectors[0]
    count = initial.shape[0]

    swap = [(i, i ^ 1) for i in range(devices)]
    below = [(s, (s + 1) % cuts) for s in range(cuts)]

    def toward(steps):
        return [(i, (i + (2 * steps if i % 2 == 0 else -2 * steps)) % devices) for i in range(devices)]

    nearer, farther = toward(1), toward(2)
    span = 2 * REACH + pair
    places = len(sent_slots(rows))
    shapes = tuple(
        jax.ShapeDtypeStruct((depth * width, whole), BF16) for depth in (pair, pair, rows) for _ in range(2)
    )
    vec = jax.ShapeDtypeStruct((count, whole), F32)

    beside = lax.ppermute(initial, "row", swap)
    sent = call(
        functools.partial(gather_kernel, rows=rows, stored=stored, total=total),
        jax.ShapeDtypeStruct((places, rows, width, width), F32),
        [HBM, HBM],
        VMEM,
        scratch_shapes=[
            pltpu.SMEM((rows, stored), jnp.int32),
            pltpu.SMEM((span,), jnp.int32),
            pltpu.SMEM((1,), jnp.int32),
            pltpu.SemaphoreType.DMA((2,)),
        ],
        cost_estimate=pl.CostEstimate(flops=0, bytes_accessed=8 * 10**6, transcendentals=0),
    )(*(pltpu.with_memory_space_constraint(array, pltpu.HBM) for array in (tile_pattern, block_tiles)))
    sent, beside = lax.optimization_barrier((sent, beside))
    received = lax.ppermute(sent, "row", swap)
    weights = call(
        functools.partial(own_weights_kernel, rows=rows, stored=stored, total=total),
        shapes,
        [HBM, VMEM],
        (VMEM,) * 6,
        scratch_shapes=[
            pltpu.SMEM((rows, stored), jnp.int32),
            pltpu.SMEM((rows * span,), jnp.int32),
            pltpu.SemaphoreType.DMA,
        ],
    )(pltpu.with_memory_space_constraint(tile_pattern, pltpu.HBM), block_tiles)
    weights = call(
        functools.partial(other_weights_kernel, rows=rows),
        shapes,
        [VMEM] * 7,
        (VMEM,) * 6,
        input_output_aliases={1 + i: i for i in range(6)},
    )(received, *weights)
    near_weights, far_weights, own_weights = weights[:2], weights[2:4], weights[4:]

    def part(kernel, group, *vectors):
        high, low = group
        depth = high.shape[0]
        return call(
            kernel,
            vec,
            [VMEM] * (len(vectors) + 2),
            VMEM,
            cost_estimate=pl.CostEstimate(
                flops=6 * count * depth * whole, bytes_accessed=4 * depth * whole, transcendentals=0
            ),
        )(*vectors, high, low)

    def apply_part(vectors, after):
        near = lax.ppermute(vectors, "row", nearer)
        far = lax.ppermute(vectors, "row", farther)
        partial = part(own_kernel, own_weights, vectors, after)
        partial = part(add_kernel, far_weights, far, partial)
        return part(add_kernel, near_weights, near, partial)

    current = call(functools.partial(join_kernel, half=half), vec, [VMEM, VMEM], VMEM)(initial, beside)
    def images(vectors, after):
        partial = apply_part(vectors, after)
        return partial, lax.ppermute(partial, "row", swap)

    def step(kernel, out_shape, *operands):
        out_specs = VMEM if out_shape is vec else (VMEM,) * len(out_shape)
        return call(functools.partial(kernel, half=half), out_shape, [VMEM] * len(operands), out_specs)(*operands)

    factors = jnp.broadcast_to(jnp.concatenate([1.0 / halfwidths, centers / halfwidths])[:, None], (2, 128))
    image = step(image_kernel, vec, *images(current, current))
    previous, current = step(second_kernel, (vec, vec), factors, *images(image, image), image, current)
    small = jax.ShapeDtypeStruct((count, count), F32)
    chosen = call(chosen_kernel, small, [SMEM, VMEM], VMEM)(dup_pairs[0].T, image)
    for _ in range(DEG - 2):
        previous, current = current, step(step_kernel, vec, factors, *images(current, chosen), current, previous)

    own = current[:, :half]
    lower = lax.ppermute(own, "cuts", below)
    partial = apply_part(current, chosen)
    lower, partial = lax.optimization_barrier((lower, partial))
    squares = call(functools.partial(gram_kernel, half=half), (small,) * 3, [VMEM, VMEM], (VMEM,) * 3)(current, lower)
    sums = jax.ShapeDtypeStruct((count, 4 * count), F32)
    products = call(cross_kernel, sums, [VMEM] * 5, VMEM)(current, partial, *squares)
    beside = lax.ppermute(products, "row", swap)
    spread = call(spread_kernel, jax.ShapeDtypeStruct((chips, *sums.shape), F32), [VMEM, VMEM], VMEM)(products, beside)
    same_core = [[2 * chip + core for chip in range(chips)] for core in range(2)]
    parts = lax.all_to_all(spread, "row", 0, 0, tiled=True, axis_index_groups=same_core)
    filtered, projected = call(
        functools.partial(finish_kernel, order=total * width),
        (jax.ShapeDtypeStruct((count, half), F32), small),
        [VMEM] * 4,
        (VMEM, VMEM),
    )(parts, chosen, own, lower)
    return (filtered[None], projected[None])


def solution(mesh):
    in_specs = (
        P("row", None, None, None),
        P("row", None),
        P("cuts", None, "row"),
        P("cuts"),
        P("cuts"),
        P("cuts", None, None),
    )
    out_specs = (P("cuts", None, "row"), P("cuts", None, None))
    return jax.shard_map(local, mesh=mesh, in_specs=in_specs, out_specs=out_specs, check_vma=False)
```

```python
import functools
import math

import jax
import jax.numpy as jnp
from jax import lax
from jax.experimental import pallas as pl
from jax.experimental.pallas import tpu as pltpu
from jax.sharding import PartitionSpec as P

DEG = 8
REACH = 12
F32 = jnp.float32
BF16 = jnp.bfloat16
NN = (((1,), (0,)), ((), ()))
NT = (((1,), (1,)), ((), ()))
VMEM = pl.BlockSpec(memory_space=pltpu.VMEM)
SMEM = pl.BlockSpec(memory_space=pltpu.SMEM)
HBM = pl.BlockSpec(memory_space=pltpu.HBM)
PARAMS = pltpu.CompilerParams(vmem_limit_bytes=24 * 2**20)


def column_of(slot, core, rows):
    pair = 2 * rows
    if slot >= 2 * pair:
        return core * rows + slot - 2 * pair
    chip, block = divmod(slot, pair)
    natural = (block + core * rows) % pair
    return natural - (chip + 1) * pair if core == 0 else natural + (chip + 1) * pair


def sent_slots(rows):
    pair = 2 * rows
    return [s for s in range(5 * rows) if not pair <= s < pair + rows]


def offset_in_span(block, start, total):
    offset = block - start
    offset = jnp.where(offset < 0, offset + total, offset)
    return jnp.where(offset >= total, offset - total, offset)


def gather_kernel(pattern, tiles, sent, blocks, places, count, sems, *, rows, stored, total):
    pair = 2 * rows
    span = 2 * REACH + pair
    copy = pltpu.make_async_copy(pattern, blocks, sems.at[0])
    copy.start()
    me = lax.axis_index("row")
    core = me % 2
    start = (me // 2) * pair - REACH
    for offset in range(span):
        places[offset] = -1
    for place, slot in enumerate(sent_slots(rows)):
        column = jnp.where(core == 0, column_of(slot, 1, rows), column_of(slot, 0, rows))
        places[column + REACH] = place
    count[0] = 0
    sent[...] = jnp.zeros_like(sent)
    copy.wait()
    for row in range(rows):
        for k in range(stored):
            place = places[offset_in_span(blocks[row, k], start, total)]

            @pl.when(place >= 0)
            def _():
                count[0] += 1
                pltpu.make_async_copy(tiles.at[row, k], sent.at[place, row], sems.at[1]).start()

    @pl.loop(0, count[0])
    def _(_):
        pltpu.make_async_copy(tiles.at[0, 0], sent.at[0, 0], sems.at[1]).wait()


def place_of(slot, rows):
    return divmod(slot, 2 * rows)


def store_tile(tile, high, low, place, lane):
    tile = tile.T
    top = tile.astype(BF16)
    rest = (tile - top.astype(F32)).astype(BF16)
    width = tile.shape[0]
    high[place * width : (place + 1) * width, lane * width : (lane + 1) * width] = top
    low[place * width : (place + 1) * width, lane * width : (lane + 1) * width] = rest


def own_weights_kernel(pattern, tiles, *refs, rows, stored, total):
    weights, (blocks, table, held, sems) = refs[:6], refs[6:]
    copies = [pltpu.make_async_copy(tiles.at[row], held.at[row], sems.at[row]) for row in range(rows)]
    copies.append(pltpu.make_async_copy(pattern, blocks, sems.at[rows]))
    for copy in reversed(copies):
        copy.start()
    span = 2 * REACH + 2 * rows
    me = lax.axis_index("row")
    core = me % 2
    start = (me // 2) * 2 * rows - REACH
    for entry in range(rows * span):
        table[entry] = -1
    copies[rows].wait()
    for row in range(rows):
        for k in range(stored):
            table[row * span + offset_in_span(blocks[row, k], start, total)] = k
    for row in reversed(range(rows)):
        copies[row].wait()
        for slot in range(5 * rows):
            group, place = place_of(slot, rows)
            column = jnp.where(core == 0, column_of(slot, 0, rows), column_of(slot, 1, rows))
            k = table[row * span + column + REACH]
            tile = held[row, jnp.maximum(k, 0)]
            store_tile(jnp.where(k >= 0, tile, 0.0), *weights[2 * group : 2 * group + 2], place, row)


def other_weights_kernel(received, *refs, rows):
    weights = refs[len(refs) // 2 :]
    places = sent_slots(rows)
    width = received.shape[2]
    for slot in range(5 * rows):
        group, place = place_of(slot, rows)
        for row in range(rows):
            if slot in places:
                tile = received[places.index(slot), row]
            else:
                tile = jnp.zeros((width, width), F32)
            store_tile(tile, *weights[2 * group : 2 * group + 2], place, rows + row)


def multiply(vectors, high, low):
    count = vectors.shape[0]
    top = vectors.astype(BF16)
    rest = (vectors - top.astype(F32)).astype(BF16)
    both = jnp.concatenate([top, rest], axis=0)
    by_high = lax.dot_general(both, high[...], NN, preferred_element_type=F32)
    by_low = lax.dot_general(top, low[...], NN, preferred_element_type=F32)
    return by_high[:count] + (by_high[count:] + by_low)


def own_kernel(vectors, _after, high, low, out):
    out[...] = multiply(vectors[:, : high.shape[0]], high, low)


def add_kernel(vectors, before, high, low, out):
    out[...] = before[...] + multiply(vectors[...], high, low)


def join_kernel(first, second, out, *, half):
    out[:, :half] = first[...]
    out[:, half:] = second[...]


def halves(partial, other, half):
    yield slice(0, half), partial[:, :half] + other[:, half:]
    yield slice(half, 2 * half), partial[:, half:] + other[:, :half]


def image_kernel(partial, other, out, *, half):
    for lanes, image in halves(partial, other, half):
        out[:, lanes] = image


def second_kernel(factors, partial, other, image, initial, first, second, *, half):
    scale = factors[0:1, 0:1]
    shift = factors[1:2, 0:1]
    for lanes, twice in halves(partial, other, half):
        once = image[:, lanes]
        start = initial[:, lanes]
        value = scale * once - shift * start
        first[:, lanes] = value
        second[:, lanes] = 2.0 * (scale * (scale * twice - shift * once) - shift * value) - start


def step_kernel(factors, partial, other, current, previous, out, *, half):
    scale = factors[0:1, 0:1]
    shift = factors[1:2, 0:1]
    for lanes, image in halves(partial, other, half):
        out[:, lanes] = 2.0 * (scale * image - shift * current[:, lanes]) - previous[:, lanes]


def dot(a, b, dims):
    return lax.dot_general(a, b, dims, precision=lax.Precision.HIGHEST, preferred_element_type=F32)


def chosen_kernel(pairs, _after, out):
    row = lax.broadcasted_iota(jnp.int32, out.shape, 0)
    column = lax.broadcasted_iota(jnp.int32, out.shape, 1)
    total = jnp.zeros(out.shape, F32)
    for p in range(pairs.shape[1]):
        total = total + ((row == pairs[0, p]) & (column == pairs[1, p])).astype(F32)
    out[...] = jnp.where(lax.axis_index("cuts") == 0, 0.0, total)


def products_kernel(vectors, before, high, low, pair, lower, out, *, half):
    own = pair[:, :half]
    below = lower[...]
    partial = before[...] + multiply(vectors[...], high, low)
    out[...] = jnp.concatenate(
        [dot(own, own, NT), dot(own, below, NT), dot(below, below, NT), dot(pair[...], partial, NT)], axis=1
    )


def spread_kernel(one, other, out):
    both = one[...] + other[...]
    for chip in range(out.shape[0]):
        out[chip] = both


def summed(parts):
    total = parts[0]
    for device in range(1, parts.shape[0]):
        total = total + parts[device]
    return total


def inverses(squares):
    count = squares.shape[0]
    block = 16
    sub = lax.broadcasted_iota(jnp.int32, squares.shape, 0)
    lane = lax.broadcasted_iota(jnp.int32, squares.shape, 1)
    left = lane < 2 * count
    place = jnp.where(left, lane, lane - 2 * count)
    work = jnp.where(place < count, squares, (place == sub + count).astype(F32))
    for k in range(0, count, block):
        columns = [
            jnp.where(left, work[:, m : m + 1], work[:, 2 * count + m : 2 * count + m + 1]) for m in range(k, k + block)
        ]
        for i in range(block):
            here = slice(k + i, k + i + 1)
            factor = jnp.where(sub > k + i, columns[i] * (1.0 / columns[i][here]), 0.0)
            for j in range(i + 1, block):
                columns[j] = columns[j] - factor * columns[j][here]
            work = work - factor * work[here]
    pivots = jnp.where(place == sub, work, 0.0)
    for start in (0, 2 * count):
        pivot = jnp.sum(pivots[:, start : start + count], axis=1, keepdims=True)
        yield work[:, start + count : start + 2 * count] * (1.0 / jnp.sqrt(pivot))


def finish_kernel(parts, chosen, vectors, lower, filtered, projected, *, order):
    count = vectors.shape[0]
    total = summed(parts)
    mixed, cross = total[:, count : 2 * count], total[:, 3 * count :]
    inverse, inverse_below = inverses(total)
    scale = math.sqrt(order)
    basis = scale * dot(inverse, vectors[...], NN)
    lower_basis = scale * dot(inverse_below, lower[...], NN)
    correlation = dot(dot(inverse, mixed, NN), inverse_below, NT)
    projected[...] = dot(dot(inverse, cross, NN), inverse, NT)
    some = jnp.max(chosen[...]) > 0.0
    removal = jnp.where(some, dot(chosen[...] * correlation, lower_basis, NN), 0.0)
    filtered[...] = basis - removal


def call(kernel, out_shape, in_specs, out_specs, **options):
    options.setdefault("compiler_params", PARAMS)
    options.setdefault("cost_estimate", pl.CostEstimate(flops=10**6, bytes_accessed=10**5, transcendentals=0))
    return pl.pallas_call(kernel, out_shape=out_shape, in_specs=in_specs, out_specs=out_specs, **options)


def local(block_tiles, tile_pattern, start_vectors, centers, halfwidths, dup_pairs):
    rows, stored, width, _ = block_tiles.shape
    devices = lax.axis_size("row")
    cuts = lax.axis_size("cuts")
    chips = devices // 2
    total = rows * devices
    pair = 2 * rows
    half = rows * width
    whole = 2 * half
    initial = start_vectors[0]
    count = initial.shape[0]

    swap = [(i, i ^ 1) for i in range(devices)]
    below = [(s, (s + 1) % cuts) for s in range(cuts)]

    def toward(steps):
        return [(i, (i + (2 * steps if i % 2 == 0 else -2 * steps)) % devices) for i in range(devices)]

    nearer, farther = toward(1), toward(2)
    span = 2 * REACH + pair
    places = len(sent_slots(rows))
    shapes = tuple(
        jax.ShapeDtypeStruct((depth * width, whole), BF16) for depth in (pair, pair, rows) for _ in range(2)
    )
    vec = jax.ShapeDtypeStruct((count, whole), F32)

    in_hbm = [pltpu.with_memory_space_constraint(array, pltpu.HBM) for array in (tile_pattern, block_tiles)]
    beside = lax.ppermute(initial, "row", swap)
    sent = call(
        functools.partial(gather_kernel, rows=rows, stored=stored, total=total),
        jax.ShapeDtypeStruct((places, rows, width, width), F32),
        [HBM, HBM],
        VMEM,
        scratch_shapes=[
            pltpu.SMEM((rows, stored), jnp.int32),
            pltpu.SMEM((span,), jnp.int32),
            pltpu.SMEM((1,), jnp.int32),
            pltpu.SemaphoreType.DMA((2,)),
        ],
        cost_estimate=pl.CostEstimate(flops=0, bytes_accessed=8 * 10**6, transcendentals=0),
    )(*in_hbm)
    sent, beside = lax.optimization_barrier((sent, beside))
    received = lax.ppermute(sent, "row", swap)
    weights = call(
        functools.partial(own_weights_kernel, rows=rows, stored=stored, total=total),
        shapes,
        [HBM, HBM],
        (VMEM,) * 6,
        scratch_shapes=[
            pltpu.SMEM((rows, stored), jnp.int32),
            pltpu.SMEM((rows * span,), jnp.int32),
            pltpu.VMEM(block_tiles.shape, F32),
            pltpu.SemaphoreType.DMA((rows + 1,)),
        ],
    )(*in_hbm)
    weights = call(
        functools.partial(other_weights_kernel, rows=rows),
        shapes,
        [VMEM] * 7,
        (VMEM,) * 6,
        input_output_aliases={1 + i: i for i in range(6)},
    )(received, *weights)
    near_weights, far_weights, own_weights = weights[:2], weights[2:4], weights[4:]

    def part(kernel, group, *vectors):
        high, low = group
        depth = high.shape[0]
        return call(
            kernel,
            vec,
            [VMEM] * (len(vectors) + 2),
            VMEM,
            cost_estimate=pl.CostEstimate(
                flops=6 * count * depth * whole, bytes_accessed=4 * depth * whole, transcendentals=0
            ),
        )(*vectors, high, low)

    def most_of_image(vectors, after):
        near = lax.ppermute(vectors, "row", nearer)
        far = lax.ppermute(vectors, "row", farther)
        partial = part(own_kernel, own_weights, vectors, after)
        return near, part(add_kernel, far_weights, far, partial)

    current = call(functools.partial(join_kernel, half=half), vec, [VMEM, VMEM], VMEM)(initial, beside)
    def images(vectors, after):
        partial = part(add_kernel, near_weights, *most_of_image(vectors, after))
        return partial, lax.ppermute(partial, "row", swap)

    def step(kernel, out_shape, *operands):
        out_specs = VMEM if out_shape is vec else (VMEM,) * len(out_shape)
        return call(functools.partial(kernel, half=half), out_shape, [VMEM] * len(operands), out_specs)(*operands)

    factors = jnp.broadcast_to(jnp.concatenate([1.0 / halfwidths, centers / halfwidths])[:, None], (2, 128))
    image = step(image_kernel, vec, *images(current, current))
    previous, current = step(second_kernel, (vec, vec), factors, *images(image, image), image, current)
    small = jax.ShapeDtypeStruct((count, count), F32)
    chosen = call(chosen_kernel, small, [SMEM, VMEM], VMEM)(dup_pairs[0].T, image)
    for _ in range(DEG - 2):
        previous, current = current, step(step_kernel, vec, factors, *images(current, chosen), current, previous)

    own = current[:, :half]
    lower = lax.ppermute(own, "cuts", below)
    near, partial = most_of_image(current, chosen)
    sums = jax.ShapeDtypeStruct((count, 4 * count), F32)
    products = call(functools.partial(products_kernel, half=half), sums, [VMEM] * 6, VMEM)(
        near, partial, *near_weights, current, lower
    )
    beside = lax.ppermute(products, "row", swap)
    spread = call(spread_kernel, jax.ShapeDtypeStruct((chips, *sums.shape), F32), [VMEM, VMEM], VMEM)(products, beside)
    same_core = [[2 * chip + core for chip in range(chips)] for core in range(2)]
    parts = lax.all_to_all(spread, "row", 0, 0, tiled=True, axis_index_groups=same_core)
    filtered, projected = call(
        functools.partial(finish_kernel, order=total * width),
        (jax.ShapeDtypeStruct((count, half), F32), small),
        [VMEM] * 4,
        (VMEM, VMEM),
    )(parts, chosen, own, lower)
    return (filtered[None], projected[None])


def solution(mesh):
    in_specs = (
        P("row", None, None, None),
        P("row", None),
        P("cuts", None, "row"),
        P("cuts"),
        P("cuts"),
        P("cuts", None, None),
    )
    out_specs = (P("cuts", None, "row"), P("cuts", None, None))
    return jax.shard_map(local, mesh=mesh, in_specs=in_specs, out_specs=out_specs, check_vma=False)
```

```python
import functools
import math

import jax
import jax.numpy as jnp
from jax import lax
from jax.experimental import pallas as pl
from jax.experimental.pallas import tpu as pltpu
from jax.sharding import PartitionSpec as P

DEG = 8
REACH = 12
F32 = jnp.float32
BF16 = jnp.bfloat16
NN = (((1,), (0,)), ((), ()))
NT = (((1,), (1,)), ((), ()))
VMEM = pl.BlockSpec(memory_space=pltpu.VMEM)
SMEM = pl.BlockSpec(memory_space=pltpu.SMEM)
HBM = pl.BlockSpec(memory_space=pltpu.HBM)
PARAMS = pltpu.CompilerParams(vmem_limit_bytes=24 * 2**20)


def column_of(slot, core, rows):
    pair = 2 * rows
    if slot >= 2 * pair:
        return core * rows + slot - 2 * pair
    chip, block = divmod(slot, pair)
    natural = (block + core * rows) % pair
    return natural - (chip + 1) * pair if core == 0 else natural + (chip + 1) * pair


def sent_slots(rows):
    pair = 2 * rows
    return [s for s in range(5 * rows) if not pair <= s < pair + rows]


def offset_in_span(block, start, total):
    offset = block - start
    offset = jnp.where(offset < 0, offset + total, offset)
    return jnp.where(offset >= total, offset - total, offset)


def gather_kernel(pattern, tiles, sent, blocks, places, count, sems, *, rows, stored, total):
    pair = 2 * rows
    span = 2 * REACH + pair
    copy = pltpu.make_async_copy(pattern, blocks, sems.at[0])
    copy.start()
    me = lax.axis_index("row")
    core = me % 2
    start = (me // 2) * pair - REACH
    for offset in range(span):
        places[offset] = -1
    for place, slot in enumerate(sent_slots(rows)):
        column = jnp.where(core == 0, column_of(slot, 1, rows), column_of(slot, 0, rows))
        places[column + REACH] = place
    count[0] = 0
    sent[...] = jnp.zeros_like(sent)
    copy.wait()
    for row in range(rows):
        for k in range(stored):
            place = places[offset_in_span(blocks[row, k], start, total)]

            @pl.when(place >= 0)
            def _():
                count[0] += 1
                pltpu.make_async_copy(tiles.at[row, k], sent.at[place, row], sems.at[1]).start()

    @pl.loop(0, count[0])
    def _(_):
        pltpu.make_async_copy(tiles.at[0, 0], sent.at[0, 0], sems.at[1]).wait()


def place_of(slot, rows):
    return divmod(slot, 2 * rows)


def store_tile(tile, high, low, place, lane):
    tile = tile.T
    top = tile.astype(BF16)
    rest = (tile - top.astype(F32)).astype(BF16)
    width = tile.shape[0]
    high[place * width : (place + 1) * width, lane * width : (lane + 1) * width] = top
    low[place * width : (place + 1) * width, lane * width : (lane + 1) * width] = rest


def own_weights_kernel(pattern, tiles, *refs, rows, stored, total):
    weights, (blocks, table, sem) = refs[:6], refs[6:]
    copy = pltpu.make_async_copy(pattern, blocks, sem)
    copy.start()
    span = 2 * REACH + 2 * rows
    me = lax.axis_index("row")
    core = me % 2
    start = (me // 2) * 2 * rows - REACH
    for entry in range(rows * span):
        table[entry] = -1
    copy.wait()
    for row in range(rows):
        for k in range(stored):
            table[row * span + offset_in_span(blocks[row, k], start, total)] = k
    for slot in range(5 * rows):
        group, place = place_of(slot, rows)
        for row in range(rows):
            column = jnp.where(core == 0, column_of(slot, 0, rows), column_of(slot, 1, rows))
            k = table[row * span + column + REACH]
            tile = tiles[row, jnp.maximum(k, 0)]
            store_tile(jnp.where(k >= 0, tile, 0.0), *weights[2 * group : 2 * group + 2], place, row)


def other_weights_kernel(received, *refs, rows):
    weights = refs[len(refs) // 2 :]
    places = sent_slots(rows)
    width = received.shape[2]
    for slot in range(5 * rows):
        group, place = place_of(slot, rows)
        for row in range(rows):
            if slot in places:
                tile = received[places.index(slot), row]
            else:
                tile = jnp.zeros((width, width), F32)
            store_tile(tile, *weights[2 * group : 2 * group + 2], place, rows + row)


def multiply(vectors, high, low):
    count = vectors.shape[0]
    top = vectors.astype(BF16)
    rest = (vectors - top.astype(F32)).astype(BF16)
    both = jnp.concatenate([top, rest], axis=0)
    by_high = lax.dot_general(both, high[...], NN, preferred_element_type=F32)
    by_low = lax.dot_general(top, low[...], NN, preferred_element_type=F32)
    return by_high[:count] + (by_high[count:] + by_low)


def own_kernel(vectors, _after, high, low, out):
    out[...] = multiply(vectors[:, : high.shape[0]], high, low)


def add_kernel(vectors, before, high, low, out):
    out[...] = before[...] + multiply(vectors[...], high, low)


def join_kernel(first, second, out, *, half):
    out[:, :half] = first[...]
    out[:, half:] = second[...]


def halves(partial, other, half):
    yield slice(0, half), partial[:, :half] + other[:, half:]
    yield slice(half, 2 * half), partial[:, half:] + other[:, :half]


def image_kernel(partial, other, out, *, half):
    for lanes, image in halves(partial, other, half):
        out[:, lanes] = image


def second_kernel(factors, partial, other, image, initial, first, second, *, half):
    scale = factors[0:1, 0:1]
    shift = factors[1:2, 0:1]
    for lanes, twice in halves(partial, other, half):
        once = image[:, lanes]
        start = initial[:, lanes]
        value = scale * once - shift * start
        first[:, lanes] = value
        second[:, lanes] = 2.0 * (scale * (scale * twice - shift * once) - shift * value) - start


def step_kernel(factors, partial, other, current, previous, out, *, half):
    scale = factors[0:1, 0:1]
    shift = factors[1:2, 0:1]
    for lanes, image in halves(partial, other, half):
        out[:, lanes] = 2.0 * (scale * image - shift * current[:, lanes]) - previous[:, lanes]


def dot(a, b, dims):
    return lax.dot_general(a, b, dims, precision=lax.Precision.HIGHEST, preferred_element_type=F32)


def chosen_kernel(pairs, _after, out):
    row = lax.broadcasted_iota(jnp.int32, out.shape, 0)
    column = lax.broadcasted_iota(jnp.int32, out.shape, 1)
    total = jnp.zeros(out.shape, F32)
    for p in range(pairs.shape[1]):
        total = total + ((row == pairs[0, p]) & (column == pairs[1, p])).astype(F32)
    out[...] = jnp.where(lax.axis_index("cuts") == 0, 0.0, total)


def products_kernel(vectors, before, high, low, pair, lower, out, *, half):
    own = pair[:, :half]
    below = lower[...]
    partial = before[...] + multiply(vectors[...], high, low)
    out[...] = jnp.concatenate(
        [dot(own, own, NT), dot(own, below, NT), dot(below, below, NT), dot(pair[...], partial, NT)], axis=1
    )


def spread_kernel(one, other, out):
    both = one[...] + other[...]
    for chip in range(out.shape[0]):
        out[chip] = both


def summed(parts):
    total = parts[0]
    for device in range(1, parts.shape[0]):
        total = total + parts[device]
    return total


def eliminated(squares):
    count = squares.shape[0]
    block = 16
    sub = lax.broadcasted_iota(jnp.int32, squares.shape, 0)
    lane = lax.broadcasted_iota(jnp.int32, squares.shape, 1)
    left = lane < 2 * count
    place = jnp.where(left, lane, lane - 2 * count)
    work = jnp.where(place < count, squares, (place == sub + count).astype(F32))
    beside = jnp.where(lane < count, pltpu.roll(squares, 3 * count, 1), pltpu.roll(squares, 2 * count, 1))
    for k in range(0, count, block):
        columns = [
            jnp.where(left, work[:, m : m + 1], work[:, 2 * count + m : 2 * count + m + 1]) for m in range(k, k + block)
        ]
        for i in range(block):
            here = slice(k + i, k + i + 1)
            factor = jnp.where(sub > k + i, columns[i] * (1.0 / columns[i][here]), 0.0)
            for j in range(i + 1, block):
                columns[j] = columns[j] - factor * columns[j][here]
            work = work - factor * work[here]
            beside = beside - factor * beside[here]
    pivots = jnp.where(place == sub, work, 0.0)
    first = 1.0 / jnp.sqrt(jnp.sum(pivots[:, :count], axis=1, keepdims=True))
    third = 1.0 / jnp.sqrt(jnp.sum(pivots[:, 2 * count : 3 * count], axis=1, keepdims=True))
    inverse = work[:, count : 2 * count] * first
    inverse_below = work[:, 3 * count :] * third
    return inverse, inverse_below, beside[:, :count] * first, beside[:, count : 2 * count] * first


def finish_kernel(parts, chosen, vectors, lower, filtered, projected, *, order):
    inverse, inverse_below, mixed, cross = eliminated(summed(parts))
    scale = math.sqrt(order)
    basis = scale * dot(inverse, vectors[...], NN)
    lower_basis = scale * dot(inverse_below, lower[...], NN)
    correlation = dot(mixed, inverse_below, NT)
    projected[...] = dot(cross, inverse, NT)
    some = jnp.max(chosen[...]) > 0.0
    removal = jnp.where(some, dot(chosen[...] * correlation, lower_basis, NN), 0.0)
    filtered[...] = basis - removal


def call(kernel, out_shape, in_specs, out_specs, **options):
    options.setdefault("compiler_params", PARAMS)
    options.setdefault("cost_estimate", pl.CostEstimate(flops=10**6, bytes_accessed=10**5, transcendentals=0))
    return pl.pallas_call(kernel, out_shape=out_shape, in_specs=in_specs, out_specs=out_specs, **options)


def local(block_tiles, tile_pattern, start_vectors, centers, halfwidths, dup_pairs):
    rows, stored, width, _ = block_tiles.shape
    devices = lax.axis_size("row")
    cuts = lax.axis_size("cuts")
    chips = devices // 2
    total = rows * devices
    pair = 2 * rows
    half = rows * width
    whole = 2 * half
    initial = start_vectors[0]
    count = initial.shape[0]

    swap = [(i, i ^ 1) for i in range(devices)]
    below = [(s, (s + 1) % cuts) for s in range(cuts)]

    def toward(steps):
        return [(i, (i + (2 * steps if i % 2 == 0 else -2 * steps)) % devices) for i in range(devices)]

    nearer, farther = toward(1), toward(2)
    span = 2 * REACH + pair
    places = len(sent_slots(rows))
    shapes = tuple(
        jax.ShapeDtypeStruct((depth * width, whole), BF16) for depth in (pair, pair, rows) for _ in range(2)
    )
    vec = jax.ShapeDtypeStruct((count, whole), F32)

    beside = lax.ppermute(initial, "row", swap)
    sent = call(
        functools.partial(gather_kernel, rows=rows, stored=stored, total=total),
        jax.ShapeDtypeStruct((places, rows, width, width), F32),
        [HBM, HBM],
        VMEM,
        scratch_shapes=[
            pltpu.SMEM((rows, stored), jnp.int32),
            pltpu.SMEM((span,), jnp.int32),
            pltpu.SMEM((1,), jnp.int32),
            pltpu.SemaphoreType.DMA((2,)),
        ],
        cost_estimate=pl.CostEstimate(flops=0, bytes_accessed=8 * 10**6, transcendentals=0),
    )(*(pltpu.with_memory_space_constraint(array, pltpu.HBM) for array in (tile_pattern, block_tiles)))
    sent, beside = lax.optimization_barrier((sent, beside))
    received = lax.ppermute(sent, "row", swap)
    weights = call(
        functools.partial(own_weights_kernel, rows=rows, stored=stored, total=total),
        shapes,
        [HBM, VMEM],
        (VMEM,) * 6,
        scratch_shapes=[
            pltpu.SMEM((rows, stored), jnp.int32),
            pltpu.SMEM((rows * span,), jnp.int32),
            pltpu.SemaphoreType.DMA,
        ],
    )(pltpu.with_memory_space_constraint(tile_pattern, pltpu.HBM), block_tiles)
    weights = call(
        functools.partial(other_weights_kernel, rows=rows),
        shapes,
        [VMEM] * 7,
        (VMEM,) * 6,
        input_output_aliases={1 + i: i for i in range(6)},
    )(received, *weights)
    near_weights, far_weights, own_weights = weights[:2], weights[2:4], weights[4:]

    def part(kernel, group, *vectors):
        high, low = group
        depth = high.shape[0]
        return call(
            kernel,
            vec,
            [VMEM] * (len(vectors) + 2),
            VMEM,
            cost_estimate=pl.CostEstimate(
                flops=6 * count * depth * whole, bytes_accessed=4 * depth * whole, transcendentals=0
            ),
        )(*vectors, high, low)

    def most_of_image(vectors, after):
        near = lax.ppermute(vectors, "row", nearer)
        far = lax.ppermute(vectors, "row", farther)
        partial = part(own_kernel, own_weights, vectors, after)
        return near, part(add_kernel, far_weights, far, partial)

    current = call(functools.partial(join_kernel, half=half), vec, [VMEM, VMEM], VMEM)(initial, beside)
    def images(vectors, after):
        partial = part(add_kernel, near_weights, *most_of_image(vectors, after))
        return partial, lax.ppermute(partial, "row", swap)

    def step(kernel, out_shape, *operands):
        out_specs = VMEM if out_shape is vec else (VMEM,) * len(out_shape)
        return call(functools.partial(kernel, half=half), out_shape, [VMEM] * len(operands), out_specs)(*operands)

    factors = jnp.broadcast_to(jnp.concatenate([1.0 / halfwidths, centers / halfwidths])[:, None], (2, 128))
    image = step(image_kernel, vec, *images(current, current))
    previous, current = step(second_kernel, (vec, vec), factors, *images(image, image), image, current)
    small = jax.ShapeDtypeStruct((count, count), F32)
    chosen = call(chosen_kernel, small, [SMEM, VMEM], VMEM)(dup_pairs[0].T, image)
    for _ in range(DEG - 2):
        previous, current = current, step(step_kernel, vec, factors, *images(current, chosen), current, previous)

    own = current[:, :half]
    lower = lax.ppermute(own, "cuts", below)
    near, partial = most_of_image(current, chosen)
    sums = jax.ShapeDtypeStruct((count, 4 * count), F32)
    products = call(functools.partial(products_kernel, half=half), sums, [VMEM] * 6, VMEM)(
        near, partial, *near_weights, current, lower
    )
    beside = lax.ppermute(products, "row", swap)
    spread = call(spread_kernel, jax.ShapeDtypeStruct((chips, *sums.shape), F32), [VMEM, VMEM], VMEM)(products, beside)
    same_core = [[2 * chip + core for chip in range(chips)] for core in range(2)]
    parts = lax.all_to_all(spread, "row", 0, 0, tiled=True, axis_index_groups=same_core)
    filtered, projected = call(
        functools.partial(finish_kernel, order=total * width),
        (jax.ShapeDtypeStruct((count, half), F32), small),
        [VMEM] * 4,
        (VMEM, VMEM),
    )(parts, chosen, own, lower)
    return (filtered[None], projected[None])


def solution(mesh):
    in_specs = (
        P("row", None, None, None),
        P("row", None),
        P("cuts", None, "row"),
        P("cuts"),
        P("cuts"),
        P("cuts", None, None),
    )
    out_specs = (P("cuts", None, "row"), P("cuts", None, None))
    return jax.shard_map(local, mesh=mesh, in_specs=in_specs, out_specs=out_specs, check_vma=False)
```

```python
import functools
import math

import jax
import jax.numpy as jnp
from jax import lax
from jax.experimental import pallas as pl
from jax.experimental.pallas import tpu as pltpu
from jax.sharding import PartitionSpec as P

DEG = 8
REACH = 12
F32 = jnp.float32
BF16 = jnp.bfloat16
NN = (((1,), (0,)), ((), ()))
NT = (((1,), (1,)), ((), ()))
VMEM = pl.BlockSpec(memory_space=pltpu.VMEM)
SMEM = pl.BlockSpec(memory_space=pltpu.SMEM)
HBM = pl.BlockSpec(memory_space=pltpu.HBM)
PARAMS = pltpu.CompilerParams(vmem_limit_bytes=24 * 2**20)


def column_of(slot, core, rows):
    pair = 2 * rows
    if slot >= 2 * pair:
        return core * rows + slot - 2 * pair
    chip, block = divmod(slot, pair)
    natural = (block + core * rows) % pair
    return natural - (chip + 1) * pair if core == 0 else natural + (chip + 1) * pair


def sent_slots(rows):
    pair = 2 * rows
    return [s for s in range(5 * rows) if not pair <= s < pair + rows]


def offset_in_span(block, start, total):
    offset = block - start
    offset = jnp.where(offset < 0, offset + total, offset)
    return jnp.where(offset >= total, offset - total, offset)


def gather_kernel(pattern, tiles, sent, blocks, places, count, sems, *, rows, stored, total):
    pair = 2 * rows
    span = 2 * REACH + pair
    copy = pltpu.make_async_copy(pattern, blocks, sems.at[0])
    copy.start()
    me = lax.axis_index("row")
    core = me % 2
    start = (me // 2) * pair - REACH
    for offset in range(span):
        places[offset] = -1
    for place, slot in enumerate(sent_slots(rows)):
        column = jnp.where(core == 0, column_of(slot, 1, rows), column_of(slot, 0, rows))
        places[column + REACH] = place
    count[0] = 0
    sent[...] = jnp.zeros_like(sent)
    copy.wait()
    for row in range(rows):
        for k in range(stored):
            place = places[offset_in_span(blocks[row, k], start, total)]

            @pl.when(place >= 0)
            def _():
                count[0] += 1
                pltpu.make_async_copy(tiles.at[row, k], sent.at[place, row], sems.at[1]).start()

    @pl.loop(0, count[0])
    def _(_):
        pltpu.make_async_copy(tiles.at[0, 0], sent.at[0, 0], sems.at[1]).wait()


def place_of(slot, rows):
    return divmod(slot, 2 * rows)


def store_tile(tile, high, low, place, lane):
    tile = tile.T
    top = tile.astype(BF16)
    rest = (tile - top.astype(F32)).astype(BF16)
    width = tile.shape[0]
    high[place * width : (place + 1) * width, lane * width : (lane + 1) * width] = top
    low[place * width : (place + 1) * width, lane * width : (lane + 1) * width] = rest


def own_weights_kernel(pattern, tiles, *refs, rows, stored, total):
    weights, (blocks, table, sem) = refs[:6], refs[6:]
    copy = pltpu.make_async_copy(pattern, blocks, sem)
    copy.start()
    span = 2 * REACH + 2 * rows
    me = lax.axis_index("row")
    core = me % 2
    start = (me // 2) * 2 * rows - REACH
    for entry in range(rows * span):
        table[entry] = -1
    copy.wait()
    for row in range(rows):
        for k in range(stored):
            table[row * span + offset_in_span(blocks[row, k], start, total)] = k
    for slot in range(5 * rows):
        group, place = place_of(slot, rows)
        for row in range(rows):
            column = jnp.where(core == 0, column_of(slot, 0, rows), column_of(slot, 1, rows))
            k = table[row * span + column + REACH]
            tile = tiles[row, jnp.maximum(k, 0)]
            store_tile(jnp.where(k >= 0, tile, 0.0), *weights[2 * group : 2 * group + 2], place, row)


def other_weights_kernel(received, *refs, rows):
    weights = refs[len(refs) // 2 :]
    places = sent_slots(rows)
    width = received.shape[2]
    for slot in range(5 * rows):
        group, place = place_of(slot, rows)
        for row in range(rows):
            if slot in places:
                tile = received[places.index(slot), row]
            else:
                tile = jnp.zeros((width, width), F32)
            store_tile(tile, *weights[2 * group : 2 * group + 2], place, rows + row)


def multiply(vectors, high, low):
    count = vectors.shape[0]
    top = vectors.astype(BF16)
    rest = (vectors - top.astype(F32)).astype(BF16)
    both = jnp.concatenate([top, rest], axis=0)
    by_high = lax.dot_general(both, high[...], NN, preferred_element_type=F32)
    by_low = lax.dot_general(top, low[...], NN, preferred_element_type=F32)
    return by_high[:count] + (by_high[count:] + by_low)


def split(values):
    top = values.astype(BF16)
    return top, (values - top.astype(F32)).astype(BF16)


def own_kernel(vectors, _after, high, low, out):
    out[...] = multiply(vectors[:, : high.shape[0]], high, low)


def add_kernel(vectors, before, high, low, out):
    out[...] = before[...] + multiply(vectors[...], high, low)


def join_kernel(first, second, out, *, half):
    out[:, :half] = first[...]
    out[:, half:] = second[...]


def halves(partial, other, half):
    yield slice(0, half), partial[:, :half] + other[:, half:]
    yield slice(half, 2 * half), partial[:, half:] + other[:, :half]


def image_kernel(partial, other, out, *, half):
    for lanes, image in halves(partial, other, half):
        out[:, lanes] = image


def second_kernel(factors, partial, other, image, initial, first, second, *, half):
    scale = factors[0:1, 0:1]
    shift = factors[1:2, 0:1]
    for lanes, twice in halves(partial, other, half):
        once = image[:, lanes]
        start = initial[:, lanes]
        value = scale * once - shift * start
        first[:, lanes] = value
        second[:, lanes] = 2.0 * (scale * (scale * twice - shift * once) - shift * value) - start


def step_kernel(factors, partial, other, current, previous, out, *, half):
    scale = factors[0:1, 0:1]
    shift = factors[1:2, 0:1]
    for lanes, image in halves(partial, other, half):
        out[:, lanes] = 2.0 * (scale * image - shift * current[:, lanes]) - previous[:, lanes]


def dot(a, b, dims):
    return lax.dot_general(a, b, dims, precision=lax.Precision.HIGHEST, preferred_element_type=F32)


def chosen_kernel(pairs, _after, out):
    row = lax.broadcasted_iota(jnp.int32, out.shape, 0)
    column = lax.broadcasted_iota(jnp.int32, out.shape, 1)
    total = jnp.zeros(out.shape, F32)
    for p in range(pairs.shape[1]):
        total = total + ((row == pairs[0, p]) & (column == pairs[1, p])).astype(F32)
    out[...] = jnp.where(lax.axis_index("cuts") == 0, 0.0, total)


def products_kernel(vectors, before, high, low, pair, lower, out, *, half):
    own = pair[:, :half]
    below = lower[...]
    partial = before[...] + multiply(vectors[...], high, low)
    out[...] = jnp.concatenate(
        [dot(own, own, NT), dot(own, below, NT), dot(below, below, NT), dot(pair[...], partial, NT)], axis=1
    )


def spread_kernel(one, other, out):
    both = one[...] + other[...]
    for chip in range(out.shape[0]):
        out[chip] = both


def summed(parts):
    total = parts[0]
    for device in range(1, parts.shape[0]):
        total = total + parts[device]
    return total


def eliminated(squares):
    count = squares.shape[0]
    block = 16
    sub = lax.broadcasted_iota(jnp.int32, squares.shape, 0)
    lane = lax.broadcasted_iota(jnp.int32, squares.shape, 1)
    left = lane < 2 * count
    place = jnp.where(left, lane, lane - 2 * count)
    work = jnp.where(place < count, squares, (place == sub + count).astype(F32))
    beside = jnp.where(lane < count, pltpu.roll(squares, 3 * count, 1), pltpu.roll(squares, 2 * count, 1))
    for k in range(0, count, block):
        columns = [
            jnp.where(left, work[:, m : m + 1], work[:, 2 * count + m : 2 * count + m + 1]) for m in range(k, k + block)
        ]
        for i in range(block):
            here = slice(k + i, k + i + 1)
            factor = jnp.where(sub > k + i, columns[i] * (1.0 / columns[i][here]), 0.0)
            for j in range(i + 1, block):
                columns[j] = columns[j] - factor * columns[j][here]
            work = work - factor * work[here]
            beside = beside - factor * beside[here]
    pivots = jnp.where(place == sub, work, 0.0)
    first = 1.0 / jnp.sqrt(jnp.sum(pivots[:, :count], axis=1, keepdims=True))
    third = 1.0 / jnp.sqrt(jnp.sum(pivots[:, 2 * count : 3 * count], axis=1, keepdims=True))
    inverse = work[:, count : 2 * count] * first
    inverse_below = work[:, 3 * count :] * third
    return inverse, inverse_below, beside[:, :count] * first, beside[:, count : 2 * count] * first


def finish_kernel(parts, chosen, vectors, lower, filtered, projected, *, order):
    inverse, inverse_below, mixed, cross = eliminated(summed(parts))
    scale = math.sqrt(order)
    basis = multiply(scale * inverse, *split(vectors[...]))
    lower_basis = multiply(scale * inverse_below, *split(lower[...]))
    correlation = dot(mixed, inverse_below, NT)
    projected[...] = dot(cross, inverse, NT)
    some = jnp.max(chosen[...]) > 0.0
    removal = jnp.where(some, multiply(chosen[...] * correlation, *split(lower_basis)), 0.0)
    filtered[...] = basis - removal


def call(kernel, out_shape, in_specs, out_specs, **options):
    options.setdefault("compiler_params", PARAMS)
    options.setdefault("cost_estimate", pl.CostEstimate(flops=10**6, bytes_accessed=10**5, transcendentals=0))
    return pl.pallas_call(kernel, out_shape=out_shape, in_specs=in_specs, out_specs=out_specs, **options)


def local(block_tiles, tile_pattern, start_vectors, centers, halfwidths, dup_pairs):
    rows, stored, width, _ = block_tiles.shape
    devices = lax.axis_size("row")
    cuts = lax.axis_size("cuts")
    chips = devices // 2
    total = rows * devices
    pair = 2 * rows
    half = rows * width
    whole = 2 * half
    initial = start_vectors[0]
    count = initial.shape[0]

    swap = [(i, i ^ 1) for i in range(devices)]
    below = [(s, (s + 1) % cuts) for s in range(cuts)]

    def toward(steps):
        return [(i, (i + (2 * steps if i % 2 == 0 else -2 * steps)) % devices) for i in range(devices)]

    nearer, farther = toward(1), toward(2)
    span = 2 * REACH + pair
    places = len(sent_slots(rows))
    shapes = tuple(
        jax.ShapeDtypeStruct((depth * width, whole), BF16) for depth in (pair, pair, rows) for _ in range(2)
    )
    vec = jax.ShapeDtypeStruct((count, whole), F32)

    beside = lax.ppermute(initial, "row", swap)
    sent = call(
        functools.partial(gather_kernel, rows=rows, stored=stored, total=total),
        jax.ShapeDtypeStruct((places, rows, width, width), F32),
        [HBM, HBM],
        VMEM,
        scratch_shapes=[
            pltpu.SMEM((rows, stored), jnp.int32),
            pltpu.SMEM((span,), jnp.int32),
            pltpu.SMEM((1,), jnp.int32),
            pltpu.SemaphoreType.DMA((2,)),
        ],
        cost_estimate=pl.CostEstimate(flops=0, bytes_accessed=8 * 10**6, transcendentals=0),
    )(*(pltpu.with_memory_space_constraint(array, pltpu.HBM) for array in (tile_pattern, block_tiles)))
    sent, beside = lax.optimization_barrier((sent, beside))
    received = lax.ppermute(sent, "row", swap)
    weights = call(
        functools.partial(own_weights_kernel, rows=rows, stored=stored, total=total),
        shapes,
        [HBM, VMEM],
        (VMEM,) * 6,
        scratch_shapes=[
            pltpu.SMEM((rows, stored), jnp.int32),
            pltpu.SMEM((rows * span,), jnp.int32),
            pltpu.SemaphoreType.DMA,
        ],
    )(pltpu.with_memory_space_constraint(tile_pattern, pltpu.HBM), block_tiles)
    weights = call(
        functools.partial(other_weights_kernel, rows=rows),
        shapes,
        [VMEM] * 7,
        (VMEM,) * 6,
        input_output_aliases={1 + i: i for i in range(6)},
    )(received, *weights)
    near_weights, far_weights, own_weights = weights[:2], weights[2:4], weights[4:]

    def part(kernel, group, *vectors):
        high, low = group
        depth = high.shape[0]
        return call(
            kernel,
            vec,
            [VMEM] * (len(vectors) + 2),
            VMEM,
            cost_estimate=pl.CostEstimate(
                flops=6 * count * depth * whole, bytes_accessed=4 * depth * whole, transcendentals=0
            ),
        )(*vectors, high, low)

    def most_of_image(vectors, after):
        near = lax.ppermute(vectors, "row", nearer)
        far = lax.ppermute(vectors, "row", farther)
        partial = part(own_kernel, own_weights, vectors, after)
        return near, part(add_kernel, far_weights, far, partial)

    current = call(functools.partial(join_kernel, half=half), vec, [VMEM, VMEM], VMEM)(initial, beside)
    def images(vectors, after):
        partial = part(add_kernel, near_weights, *most_of_image(vectors, after))
        return partial, lax.ppermute(partial, "row", swap)

    def step(kernel, out_shape, *operands):
        out_specs = VMEM if out_shape is vec else (VMEM,) * len(out_shape)
        return call(functools.partial(kernel, half=half), out_shape, [VMEM] * len(operands), out_specs)(*operands)

    factors = jnp.broadcast_to(jnp.concatenate([1.0 / halfwidths, centers / halfwidths])[:, None], (2, 128))
    image = step(image_kernel, vec, *images(current, current))
    previous, current = step(second_kernel, (vec, vec), factors, *images(image, image), image, current)
    small = jax.ShapeDtypeStruct((count, count), F32)
    chosen = call(chosen_kernel, small, [SMEM, VMEM], VMEM)(dup_pairs[0].T, image)
    for _ in range(DEG - 2):
        previous, current = current, step(step_kernel, vec, factors, *images(current, chosen), current, previous)

    own = current[:, :half]
    lower = lax.ppermute(own, "cuts", below)
    near, partial = most_of_image(current, chosen)
    sums = jax.ShapeDtypeStruct((count, 4 * count), F32)
    products = call(functools.partial(products_kernel, half=half), sums, [VMEM] * 6, VMEM)(
        near, partial, *near_weights, current, lower
    )
    beside = lax.ppermute(products, "row", swap)
    spread = call(spread_kernel, jax.ShapeDtypeStruct((chips, *sums.shape), F32), [VMEM, VMEM], VMEM)(products, beside)
    same_core = [[2 * chip + core for chip in range(chips)] for core in range(2)]
    parts = lax.all_to_all(spread, "row", 0, 0, tiled=True, axis_index_groups=same_core)
    filtered, projected = call(
        functools.partial(finish_kernel, order=total * width),
        (jax.ShapeDtypeStruct((count, half), F32), small),
        [VMEM] * 4,
        (VMEM, VMEM),
    )(parts, chosen, own, lower)
    return (filtered[None], projected[None])


def solution(mesh):
    in_specs = (
        P("row", None, None, None),
        P("row", None),
        P("cuts", None, "row"),
        P("cuts"),
        P("cuts"),
        P("cuts", None, None),
    )
    out_specs = (P("cuts", None, "row"), P("cuts", None, None))
    return jax.shard_map(local, mesh=mesh, in_specs=in_specs, out_specs=out_specs, check_vma=False)
```

```python
import functools
import math

import jax
import jax.numpy as jnp
from jax import lax
from jax.experimental import pallas as pl
from jax.experimental.pallas import tpu as pltpu
from jax.sharding import PartitionSpec as P

DEG = 8
REACH = 12
F32 = jnp.float32
BF16 = jnp.bfloat16
NN = (((1,), (0,)), ((), ()))
NT = (((1,), (1,)), ((), ()))
VMEM = pl.BlockSpec(memory_space=pltpu.VMEM)
SMEM = pl.BlockSpec(memory_space=pltpu.SMEM)
HBM = pl.BlockSpec(memory_space=pltpu.HBM)
PARAMS = pltpu.CompilerParams(vmem_limit_bytes=24 * 2**20)


def column_of(slot, core, rows):
    pair = 2 * rows
    if slot >= 2 * pair:
        return core * rows + slot - 2 * pair
    chip, block = divmod(slot, pair)
    natural = (block + core * rows) % pair
    return natural - (chip + 1) * pair if core == 0 else natural + (chip + 1) * pair


def sent_slots(rows):
    pair = 2 * rows
    return [s for s in range(5 * rows) if not pair <= s < pair + rows]


def offset_in_span(block, start, total):
    offset = block - start
    offset = jnp.where(offset < 0, offset + total, offset)
    return jnp.where(offset >= total, offset - total, offset)


def gather_kernel(pattern, tiles, sent, blocks, places, count, sems, *, rows, stored, total):
    pair = 2 * rows
    span = 2 * REACH + pair
    copy = pltpu.make_async_copy(pattern, blocks, sems.at[0])
    copy.start()
    me = lax.axis_index("row")
    core = me % 2
    start = (me // 2) * pair - REACH
    for offset in range(span):
        places[offset] = -1
    for place, slot in enumerate(sent_slots(rows)):
        column = jnp.where(core == 0, column_of(slot, 1, rows), column_of(slot, 0, rows))
        places[column + REACH] = place
    count[0] = 0
    sent[...] = jnp.zeros_like(sent)
    copy.wait()
    for row in range(rows):
        for k in range(stored):
            place = places[offset_in_span(blocks[row, k], start, total)]

            @pl.when(place >= 0)
            def _():
                count[0] += 1
                pltpu.make_async_copy(tiles.at[row, k], sent.at[place, row], sems.at[1]).start()

    @pl.loop(0, count[0])
    def _(_):
        pltpu.make_async_copy(tiles.at[0, 0], sent.at[0, 0], sems.at[1]).wait()


def place_of(slot, rows):
    return divmod(slot, 2 * rows)


def store_tile(tile, high, low, place, lane):
    tile = tile.T
    top = tile.astype(BF16)
    rest = (tile - top.astype(F32)).astype(BF16)
    width = tile.shape[0]
    high[place * width : (place + 1) * width, lane * width : (lane + 1) * width] = top
    low[place * width : (place + 1) * width, lane * width : (lane + 1) * width] = rest


def own_weights_kernel(pattern, tiles, *refs, rows, stored, total):
    weights, (blocks, table, sem) = refs[:6], refs[6:]
    copy = pltpu.make_async_copy(pattern, blocks, sem)
    copy.start()
    span = 2 * REACH + 2 * rows
    me = lax.axis_index("row")
    core = me % 2
    start = (me // 2) * 2 * rows - REACH
    for entry in range(rows * span):
        table[entry] = -1
    copy.wait()
    for row in range(rows):
        for k in range(stored):
            table[row * span + offset_in_span(blocks[row, k], start, total)] = k
    for slot in range(5 * rows):
        group, place = place_of(slot, rows)
        for row in range(rows):
            column = jnp.where(core == 0, column_of(slot, 0, rows), column_of(slot, 1, rows))
            k = table[row * span + column + REACH]
            tile = tiles[row, jnp.maximum(k, 0)]
            store_tile(jnp.where(k >= 0, tile, 0.0), *weights[2 * group : 2 * group + 2], place, row)


def other_weights_kernel(received, *refs, rows):
    weights = refs[len(refs) // 2 :]
    places = sent_slots(rows)
    width = received.shape[2]
    for slot in range(5 * rows):
        group, place = place_of(slot, rows)
        for row in range(rows):
            if slot in places:
                tile = received[places.index(slot), row]
            else:
                tile = jnp.zeros((width, width), F32)
            store_tile(tile, *weights[2 * group : 2 * group + 2], place, rows + row)


def multiply(vectors, high, low):
    count = vectors.shape[0]
    top = vectors.astype(BF16)
    rest = (vectors - top.astype(F32)).astype(BF16)
    both = jnp.concatenate([top, rest], axis=0)
    by_high = lax.dot_general(both, high[...], NN, preferred_element_type=F32)
    by_low = lax.dot_general(top, low[...], NN, preferred_element_type=F32)
    return by_high[:count] + (by_high[count:] + by_low)


def own_kernel(vectors, _after, high, low, out):
    out[...] = multiply(vectors[:, : high.shape[0]], high, low)


def add_kernel(vectors, before, high, low, out):
    out[...] = before[...] + multiply(vectors[...], high, low)


def join_kernel(first, second, out, *, half):
    out[:, :half] = first[...]
    out[:, half:] = second[...]


def halves(partial, other, half):
    yield slice(0, half), partial[:, :half] + other[:, half:]
    yield slice(half, 2 * half), partial[:, half:] + other[:, :half]


def image_kernel(partial, other, out, *, half):
    for lanes, image in halves(partial, other, half):
        out[:, lanes] = image


def second_kernel(factors, partial, other, image, initial, first, second, *, half):
    scale = factors[0:1, 0:1]
    shift = factors[1:2, 0:1]
    for lanes, twice in halves(partial, other, half):
        once = image[:, lanes]
        start = initial[:, lanes]
        value = scale * once - shift * start
        first[:, lanes] = value
        second[:, lanes] = 2.0 * (scale * (scale * twice - shift * once) - shift * value) - start


def step_kernel(factors, partial, other, current, previous, out, *, half):
    scale = factors[0:1, 0:1]
    shift = factors[1:2, 0:1]
    for lanes, image in halves(partial, other, half):
        out[:, lanes] = 2.0 * (scale * image - shift * current[:, lanes]) - previous[:, lanes]


def dot(a, b, dims):
    return lax.dot_general(a, b, dims, precision=lax.Precision.HIGHEST, preferred_element_type=F32)


def chosen_kernel(pairs, _after, out):
    row = lax.broadcasted_iota(jnp.int32, out.shape, 0)
    column = lax.broadcasted_iota(jnp.int32, out.shape, 1)
    total = jnp.zeros(out.shape, F32)
    for p in range(pairs.shape[1]):
        total = total + ((row == pairs[0, p]) & (column == pairs[1, p])).astype(F32)
    out[...] = jnp.where(lax.axis_index("cuts") == 0, 0.0, total)


def products_kernel(vectors, before, high, low, pair, lower, out, *, half):
    own = pair[:, :half]
    below = lower[...]
    partial = before[...] + multiply(vectors[...], high, low)
    out[...] = jnp.concatenate(
        [dot(own, own, NT), dot(own, below, NT), dot(below, below, NT), dot(pair[...], partial, NT)], axis=1
    )


def spread_kernel(one, other, out):
    both = one[...] + other[...]
    for chip in range(out.shape[0]):
        out[chip] = both


def summed(parts):
    total = parts[0]
    for device in range(1, parts.shape[0]):
        total = total + parts[device]
    return total


def eliminated(squares):
    count = squares.shape[0]
    block = 16
    sub = lax.broadcasted_iota(jnp.int32, squares.shape, 0)
    lane = lax.broadcasted_iota(jnp.int32, squares.shape, 1)
    left = lane < 2 * count
    place = jnp.where(left, lane, lane - 2 * count)
    work = jnp.where(place < count, squares, (place == sub + count).astype(F32))
    beside = jnp.where(lane < count, pltpu.roll(squares, 3 * count, 1), pltpu.roll(squares, 2 * count, 1))
    for k in range(0, count, block):
        columns = [
            jnp.where(left, work[:, m : m + 1], work[:, 2 * count + m : 2 * count + m + 1]) for m in range(k, k + block)
        ]
        for i in range(block):
            here = slice(k + i, k + i + 1)
            factor = jnp.where(sub > k + i, columns[i] * (1.0 / columns[i][here]), 0.0)
            for j in range(i + 1, block):
                columns[j] = columns[j] - factor * columns[j][here]
            work = work - factor * work[here]
            beside = beside - factor * beside[here]
    pivots = jnp.where(place == sub, work, 0.0)
    first = 1.0 / jnp.sqrt(jnp.sum(pivots[:, :count], axis=1, keepdims=True))
    third = 1.0 / jnp.sqrt(jnp.sum(pivots[:, 2 * count : 3 * count], axis=1, keepdims=True))
    inverse = work[:, count : 2 * count] * first
    inverse_below = work[:, 3 * count :] * third
    return inverse, inverse_below, beside[:, :count] * first, beside[:, count : 2 * count] * first


def finish_kernel(parts, chosen, vectors, lower, filtered, projected, *, order):
    inverse, inverse_below, mixed, cross = eliminated(summed(parts))
    scale = math.sqrt(order)
    basis = scale * dot(inverse, vectors[...], NN)
    lower_basis = scale * dot(inverse_below, lower[...], NN)
    correlation = dot(mixed, inverse_below, NT)
    projected[...] = dot(cross, inverse, NT)
    some = lax.axis_index("cuts") > 0
    removal = jnp.where(some, dot(chosen[...] * correlation, lower_basis, NN), 0.0)
    filtered[...] = basis - removal


def call(kernel, out_shape, in_specs, out_specs, **options):
    options.setdefault("compiler_params", PARAMS)
    options.setdefault("cost_estimate", pl.CostEstimate(flops=10**6, bytes_accessed=10**5, transcendentals=0))
    return pl.pallas_call(kernel, out_shape=out_shape, in_specs=in_specs, out_specs=out_specs, **options)


def local(block_tiles, tile_pattern, start_vectors, centers, halfwidths, dup_pairs):
    rows, stored, width, _ = block_tiles.shape
    devices = lax.axis_size("row")
    cuts = lax.axis_size("cuts")
    chips = devices // 2
    total = rows * devices
    pair = 2 * rows
    half = rows * width
    whole = 2 * half
    initial = start_vectors[0]
    count = initial.shape[0]

    swap = [(i, i ^ 1) for i in range(devices)]
    below = [(s, (s + 1) % cuts) for s in range(cuts)]

    def toward(steps):
        return [(i, (i + (2 * steps if i % 2 == 0 else -2 * steps)) % devices) for i in range(devices)]

    nearer, farther = toward(1), toward(2)
    span = 2 * REACH + pair
    places = len(sent_slots(rows))
    shapes = tuple(
        jax.ShapeDtypeStruct((depth * width, whole), BF16) for depth in (pair, pair, rows) for _ in range(2)
    )
    vec = jax.ShapeDtypeStruct((count, whole), F32)

    beside = lax.ppermute(initial, "row", swap)
    sent = call(
        functools.partial(gather_kernel, rows=rows, stored=stored, total=total),
        jax.ShapeDtypeStruct((places, rows, width, width), F32),
        [HBM, HBM],
        VMEM,
        scratch_shapes=[
            pltpu.SMEM((rows, stored), jnp.int32),
            pltpu.SMEM((span,), jnp.int32),
            pltpu.SMEM((1,), jnp.int32),
            pltpu.SemaphoreType.DMA((2,)),
        ],
        cost_estimate=pl.CostEstimate(flops=0, bytes_accessed=8 * 10**6, transcendentals=0),
    )(*(pltpu.with_memory_space_constraint(array, pltpu.HBM) for array in (tile_pattern, block_tiles)))
    sent, beside = lax.optimization_barrier((sent, beside))
    received = lax.ppermute(sent, "row", swap)
    weights = call(
        functools.partial(own_weights_kernel, rows=rows, stored=stored, total=total),
        shapes,
        [HBM, VMEM],
        (VMEM,) * 6,
        scratch_shapes=[
            pltpu.SMEM((rows, stored), jnp.int32),
            pltpu.SMEM((rows * span,), jnp.int32),
            pltpu.SemaphoreType.DMA,
        ],
    )(pltpu.with_memory_space_constraint(tile_pattern, pltpu.HBM), block_tiles)
    weights = call(
        functools.partial(other_weights_kernel, rows=rows),
        shapes,
        [VMEM] * 7,
        (VMEM,) * 6,
        input_output_aliases={1 + i: i for i in range(6)},
    )(received, *weights)
    near_weights, far_weights, own_weights = weights[:2], weights[2:4], weights[4:]

    def part(kernel, group, *vectors):
        high, low = group
        depth = high.shape[0]
        return call(
            kernel,
            vec,
            [VMEM] * (len(vectors) + 2),
            VMEM,
            cost_estimate=pl.CostEstimate(
                flops=6 * count * depth * whole, bytes_accessed=4 * depth * whole, transcendentals=0
            ),
        )(*vectors, high, low)

    def most_of_image(vectors, after):
        near = lax.ppermute(vectors, "row", nearer)
        far = lax.ppermute(vectors, "row", farther)
        partial = part(own_kernel, own_weights, vectors, after)
        return near, part(add_kernel, far_weights, far, partial)

    current = call(functools.partial(join_kernel, half=half), vec, [VMEM, VMEM], VMEM)(initial, beside)
    def images(vectors, after):
        partial = part(add_kernel, near_weights, *most_of_image(vectors, after))
        return partial, lax.ppermute(partial, "row", swap)

    def step(kernel, out_shape, *operands):
        out_specs = VMEM if out_shape is vec else (VMEM,) * len(out_shape)
        return call(functools.partial(kernel, half=half), out_shape, [VMEM] * len(operands), out_specs)(*operands)

    factors = jnp.broadcast_to(jnp.concatenate([1.0 / halfwidths, centers / halfwidths])[:, None], (2, 128))
    image = step(image_kernel, vec, *images(current, current))
    previous, current = step(second_kernel, (vec, vec), factors, *images(image, image), image, current)
    small = jax.ShapeDtypeStruct((count, count), F32)
    chosen = call(chosen_kernel, small, [SMEM, VMEM], VMEM)(dup_pairs[0].T, image)
    for _ in range(DEG - 2):
        previous, current = current, step(step_kernel, vec, factors, *images(current, chosen), current, previous)

    own = current[:, :half]
    lower = lax.ppermute(own, "cuts", below)
    near, partial = most_of_image(current, chosen)
    sums = jax.ShapeDtypeStruct((count, 4 * count), F32)
    products = call(functools.partial(products_kernel, half=half), sums, [VMEM] * 6, VMEM)(
        near, partial, *near_weights, current, lower
    )
    beside = lax.ppermute(products, "row", swap)
    spread = call(spread_kernel, jax.ShapeDtypeStruct((chips, *sums.shape), F32), [VMEM, VMEM], VMEM)(products, beside)
    same_core = [[2 * chip + core for chip in range(chips)] for core in range(2)]
    parts = lax.all_to_all(spread, "row", 0, 0, tiled=True, axis_index_groups=same_core)
    filtered, projected = call(
        functools.partial(finish_kernel, order=total * width),
        (jax.ShapeDtypeStruct((count, half), F32), small),
        [VMEM] * 4,
        (VMEM, VMEM),
    )(parts, chosen, own, lower)
    return (filtered[None], projected[None])


def solution(mesh):
    in_specs = (
        P("row", None, None, None),
        P("row", None),
        P("cuts", None, "row"),
        P("cuts"),
        P("cuts"),
        P("cuts", None, None),
    )
    out_specs = (P("cuts", None, "row"), P("cuts", None, None))
    return jax.shard_map(local, mesh=mesh, in_specs=in_specs, out_specs=out_specs, check_vma=False)
```
